32 devices in a mesh: dp: 4 (over z), node: 8 (over y, x, core).
Axes of the slice: x: 2, y: 2, z: 4, core: 2. Of those that a mesh axis runs over, the one named last changes fastest.
Arguments:
- normed: bfloat16 [64, 4096], P(('dp', 'node')), may hold values from -6 to 6
- cotangent: bfloat16 [64, 4096], P(('dp', 'node')), may hold values from -4 to 4
- gate_weight: bfloat16 [4096, 14336], P(None, 'node'), may hold values from -0.09375 to 0.09375
- up_weight: bfloat16 [4096, 14336], P(None, 'node'), may hold values from -0.09375 to 0.09375
- down_weight: bfloat16 [14336, 4096], P('node'), may hold values from -0.046875 to 0.046875
Outputs:
- grad_normed: bfloat16 [64, 4096], P(('dp', 'node'))
- weight_grads: float32 [12288, 14336], P('dp', 'node')
The draws below stay inside these ranges and needn't reach their ends.
All inputs are finite; a program needn't handle non-finite values.
Results may differ from the reference program's by a relative error of at most 0.0085.
Values may be sent and summed in bfloat16 or wider, within the bound.
No kernel may reach another device: no remote copies, remote signals or barrier semaphores. Data moves between devices by JAX's collectives and lax.ppermute only.
A program may use at most 256 MiB of HBM per device.

```python
import jax
import jax.numpy as jnp
from jax import lax

D = 4096
FF = 14336
GROUP = 16
TOKENS = 64
N_DP = 4


def shard_levels(own_key, extent, cuts, smallest, high):
    factor_of, own = 1.0, jax.random.fold_in(own_key, 6)
    for axis_at, shards_of in cuts:
        draws = jnp.exp(jax.random.uniform(jax.random.fold_in(own, axis_at), (shards_of,), jnp.float32, smallest / len(cuts), high / len(cuts)))
        factor_of = factor_of * jnp.repeat(draws, extent[axis_at] // shards_of).reshape([-1 if axis == axis_at else 1 for axis in range(len(extent))])
    return factor_of


def gaussian(stream_key, shape, scale, bound, shards=(), dtype=jnp.bfloat16):
    gain = shard_levels(stream_key, shape, shards, -0.22, 0.18) if shards else 1.0
    values = jax.random.normal(stream_key, shape, jnp.float32) * scale * gain
    return jnp.minimum(jnp.maximum(values, -bound), bound).astype(dtype)


def setup_inputs(seed: int = 0) -> dict:
    key_of = jax.random.split(jax.random.key(seed), 6)
    return {
        "normed": gaussian(key_of[0], (TOKENS, D), 1.0, 6.0, ((0, 32),)),
        "cotangent": gaussian(key_of[1], (TOKENS, D), 0.3, 4.0, ((0, 32),)),
        "gate_weight": gaussian(key_of[2], (D, FF), D ** -0.5, 0.09375, ((1, 8),)),
        "up_weight": gaussian(key_of[3], (D, FF), D ** -0.5, 0.09375, ((1, 8),)),
        "down_weight": gaussian(key_of[4], (FF, D), FF ** -0.5, 0.046875, ((0, 8),)),
    }


def reference(normed, cotangent, gate_weight, up_weight, down_weight):
    gate_pre = jnp.dot(normed, gate_weight, preferred_element_type=jnp.float32)
    up_pre = jnp.dot(normed, up_weight, preferred_element_type=jnp.float32)
    sigma = jax.nn.sigmoid(gate_pre)
    activated = gate_pre * sigma
    hidden = (activated * up_pre).astype(jnp.bfloat16)
    grad_hidden = jnp.dot(cotangent, down_weight.T, preferred_element_type=jnp.float32)
    grad_gate = (grad_hidden * up_pre * sigma * (1.0 + gate_pre * (1.0 - sigma))).astype(jnp.bfloat16)
    grad_up = (grad_hidden * activated).astype(jnp.bfloat16)
    grad_normed = (jnp.dot(grad_gate, gate_weight.T, preferred_element_type=jnp.float32)
                   + jnp.dot(grad_up, up_weight.T, preferred_element_type=jnp.float32)).astype(jnp.bfloat16)

    def split(array):
        return array.reshape((N_DP, GROUP, array.shape[1]))

    def one_group(carry, parts):
        rows_in, rows_cot, rows_gate, rows_up, rows_hidden = parts
        stacked = jnp.concatenate([
            jnp.dot(rows_in.T, rows_gate, preferred_element_type=jnp.float32),
            jnp.dot(rows_in.T, rows_up, preferred_element_type=jnp.float32),
            jnp.dot(rows_cot.T, rows_hidden, preferred_element_type=jnp.float32)], axis=0)
        rounded = lax.optimization_barrier(stacked.astype(jnp.bfloat16))
        return carry + rounded.astype(jnp.float32), None

    start_sum = jnp.zeros((3 * D, FF), jnp.float32)
    weight_grads, unused = lax.scan(one_group, start_sum,
                                    (split(normed), split(cotangent), split(grad_gate), split(grad_up), split(hidden)))
    return grad_normed, weight_grads
```

```python
import jax
import jax.numpy as jnp
from jax import lax
from jax.experimental import pallas as pl
from jax.experimental.pallas import tpu as pltpu
from jax.sharding import PartitionSpec as P

BF = jnp.bfloat16
F32 = jnp.float32
NN = (((1,), (0,)), ((), ()))
NT = (((1,), (1,)), ((), ()))
TN = (((0,), (0,)), ((), ()))
VMEM_SPEC = pl.BlockSpec(memory_space=pltpu.VMEM)


def dot(left, right, dims):
    return lax.dot_general(left, right, dims, preferred_element_type=F32)


def in_vmem(array):
    return pltpu.with_memory_space_constraint(array, pltpu.VMEM)


def xor_pairs(count, step):
    return [(i, i ^ step) for i in range(count)]


def shards_any(n_dp, normed, cotangent, gate_weight, up_weight, down_weight):
    rows = lax.all_gather(normed, "node", axis=0, tiled=True)
    cots = lax.all_gather(cotangent, "node", axis=0, tiled=True)
    gate_pre = dot(rows, gate_weight, NN)
    up_pre = dot(rows, up_weight, NN)
    sigma = jax.nn.sigmoid(gate_pre)
    activated = gate_pre * sigma
    hidden = (activated * up_pre).astype(BF)
    grad_hidden = dot(cots, down_weight, NT)
    grad_gate = (grad_hidden * up_pre * sigma * (1.0 + gate_pre * (1.0 - sigma))).astype(BF)
    grad_up = (grad_hidden * activated).astype(BF)
    grad_normed = lax.psum_scatter(
        dot(grad_gate, gate_weight, NT) + dot(grad_up, up_weight, NT),
        "node",
        scatter_dimension=0,
        tiled=True,
    ).astype(BF)
    stacked = jnp.concatenate(
        [dot(rows, grad_gate, TN), dot(rows, grad_up, TN), dot(cots, hidden, TN)], axis=0
    )
    weight_grads = lax.psum_scatter(
        stacked.astype(BF), "dp", scatter_dimension=0, tiled=True
    ).astype(F32)
    return grad_normed, weight_grads


def forward_kernel(chunk, tokens, gate, up, down, grads):
    columns = gate.shape[1]
    for start in range(0, columns, chunk):
        part = slice(start, start + chunk)
        gate_pre = dot(tokens[0], gate[:, part], NN)
        up_pre = dot(tokens[0], up[:, part], NN)
        grad_hidden = dot(tokens[1], down[part, :], NT)
        sigma = jax.nn.sigmoid(gate_pre)
        activated = gate_pre * sigma
        grads[0, :, part] = (
            grad_hidden * up_pre * sigma * (1.0 + gate_pre * (1.0 - sigma))
        ).astype(BF)
        grads[1, :, part] = (grad_hidden * activated).astype(BF)
        grads[2, :, part] = (activated * up_pre).astype(BF)


def backward_kernel(chunk, grads, gate, up, keep, send):
    width = gate.shape[0]
    half = keep.shape[0]
    for start in range(0, width, chunk):
        part = slice(start, start + chunk)
        total = dot(grads[0], gate[part, :], NT) + dot(grads[1], up[part, :], NT)
        keep[:, part] = total[:half]
        send[:, part] = total[half:].astype(BF)


def product_kernel(row_blocks, tokens, grads, out):
    out[...] = dot(tokens[...], grads[0], TN)


def shards_group(mesh_shape, normed, cotangent, gate_weight, up_weight, down_weight):
    n_dp, n_node = mesh_shape
    own, width = normed.shape
    hidden = gate_weight.shape[1]
    group = own * n_node
    block = 3 * width // n_dp
    d = lax.axis_index("dp")
    other_chips = range(2, n_node, 2)
    groups = range(1, n_dp)

    tokens = jnp.stack([normed, cotangent])
    spread = jnp.stack(
        [tokens] + [lax.ppermute(tokens, "node", xor_pairs(n_node, s)) for s in other_chips]
    )
    spread = jnp.stack([spread, lax.ppermute(spread, "node", xor_pairs(n_node, 1))])
    group_tokens = spread.transpose(2, 0, 1, 3, 4).reshape(2, group, width)

    def columns_for(rows, owner):
        wide = jnp.concatenate([rows[0], rows[0], rows[1]], axis=-1)
        return lax.dynamic_slice_in_dim(wide, owner * block, block, axis=wide.ndim - 1)

    far = jnp.stack(
        [lax.ppermute(columns_for(tokens, d ^ s), "dp", xor_pairs(n_dp, s)) for s in groups]
    )
    far = jnp.stack([far] + [lax.ppermute(far, "node", xor_pairs(n_node, s)) for s in other_chips])
    far = jnp.stack([far, lax.ppermute(far, "node", xor_pairs(n_node, 1))])
    far = far.transpose(2, 0, 1, 3, 4).reshape((n_dp - 1) * group, block)
    columns = jnp.concatenate([columns_for(group_tokens, d), far], axis=0)

    gate, up, down = in_vmem(gate_weight), in_vmem(up_weight), in_vmem(down_weight)
    weight_bytes = 2 * width * hidden
    grads = pl.pallas_call(
        lambda *refs: forward_kernel(256, *refs),
        out_shape=jax.ShapeDtypeStruct((3, group, hidden), BF),
        in_specs=[VMEM_SPEC] * 4,
        out_specs=VMEM_SPEC,
        compiler_params=pltpu.CompilerParams(vmem_limit_bytes=6 << 20),
        cost_estimate=pl.CostEstimate(
            flops=6 * group * width * hidden, bytes_accessed=3 * weight_bytes, transcendentals=0
        ),
        name="forward",
    )(group_tokens, gate, up, down)

    def matrices_for(owner):
        first = owner * block // width
        last = (owner * block + block - 1) // width
        return jnp.stack(
            [
                lax.dynamic_index_in_dim(grads, first, 0, keepdims=False),
                lax.dynamic_index_in_dim(grads, last, 0, keepdims=False),
            ]
        )

    pairs = jnp.concatenate(
        [matrices_for(d)]
        + [lax.ppermute(matrices_for(d ^ s), "dp", xor_pairs(n_dp, s)) for s in groups],
        axis=1,
    )

    keep, send = pl.pallas_call(
        lambda *refs: backward_kernel(256, *refs),
        out_shape=(
            jax.ShapeDtypeStruct((group // 2, width), F32),
            jax.ShapeDtypeStruct((group // 2, width), BF),
        ),
        in_specs=[VMEM_SPEC] * 3,
        out_specs=(VMEM_SPEC, VMEM_SPEC),
        compiler_params=pltpu.CompilerParams(vmem_limit_bytes=6 << 20),
        cost_estimate=pl.CostEstimate(
            flops=4 * group * width * hidden, bytes_accessed=2 * weight_bytes, transcendentals=0
        ),
        name="backward",
    )(grads, gate, up)

    chip = keep + lax.ppermute(send, "node", xor_pairs(n_node, 1)).astype(F32)
    grad_normed = chip[:own]
    for slot, s in enumerate(other_chips, 1):
        piece = chip[own * slot : own * (slot + 1)].astype(BF)
        grad_normed = grad_normed + lax.ppermute(piece, "node", xor_pairs(n_node, s)).astype(F32)

    rows = 256
    per_matrix = width // rows
    step_blocks = block // rows
    base = d * step_blocks
    which = (
        (jnp.arange(step_blocks) + base) // per_matrix - base // per_matrix
    ).astype(jnp.int32)
    weight_grads = pl.pallas_call(
        product_kernel,
        out_shape=jax.ShapeDtypeStruct((block, hidden), F32),
        grid_spec=pltpu.PrefetchScalarGridSpec(
            num_scalar_prefetch=1,
            grid=(step_blocks,),
            in_specs=[
                pl.BlockSpec((n_dp * group, rows), lambda i, which: (0, i)),
                pl.BlockSpec((1, n_dp * group, hidden), lambda i, which: (which[i], 0, 0)),
            ],
            out_specs=pl.BlockSpec((rows, hidden), lambda i, which: (i, 0)),
        ),
        compiler_params=pltpu.CompilerParams(vmem_limit_bytes=16 << 20),
        cost_estimate=pl.CostEstimate(
            flops=2 * n_dp * group * block * hidden,
            bytes_accessed=4 * block * hidden,
            transcendentals=0,
        ),
        name="product",
    )(which, columns, pairs)
    return grad_normed.astype(BF), weight_grads


def solution(mesh):
    n_dp, n_node = mesh.shape["dp"], mesh.shape["node"]

    def shards(*arrays):
        normed, gate_weight = arrays[0], arrays[2]
        rows, width = normed.shape
        hidden = gate_weight.shape[1]
        fits = (
            n_dp & (n_dp - 1) == 0
            and n_node & (n_node - 1) == 0
            and 2 <= n_node <= 8
            and n_dp <= 4
            and rows * n_node == 16
            and hidden % 256 == 0
            and hidden * width * 6 <= 46 << 20
            and 3 * width % (n_dp * 256) == 0
            and 3 * width // n_dp <= width
        )
        if fits:
            return shards_group((n_dp, n_node), *arrays)
        return shards_any(n_dp, *arrays)

    in_specs = (
        P(("dp", "node"), None),
        P(("dp", "node"), None),
        P(None, "node"),
        P(None, "node"),
        P("node", None),
    )
    out_specs = (P(("dp", "node"), None), P("dp", "node"))
    return jax.shard_map(shards, mesh=mesh, in_specs=in_specs, out_specs=out_specs, check_vma=False)
```

```python
import jax
import jax.numpy as jnp
from jax import lax
from jax.experimental import pallas as pl
from jax.experimental.pallas import tpu as pltpu
from jax.sharding import PartitionSpec as P

BF = jnp.bfloat16
F32 = jnp.float32
NN = (((1,), (0,)), ((), ()))
NT = (((1,), (1,)), ((), ()))
TN = (((0,), (0,)), ((), ()))
ANY_SPEC = pl.BlockSpec(memory_space=pl.ANY)
HBM_SPEC = pl.BlockSpec(memory_space=pltpu.HBM)
VMEM_SPEC = pl.BlockSpec(memory_space=pltpu.VMEM)


def dot(left, right, dims):
    return lax.dot_general(left, right, dims, preferred_element_type=F32)


def in_hbm(array):
    return pltpu.with_memory_space_constraint(array, pltpu.HBM)


def in_vmem(array):
    return pltpu.with_memory_space_constraint(array, pltpu.VMEM)


def xor_pairs(count, step):
    return [(i, i ^ step) for i in range(count)]


def shards_any(n_dp, normed, cotangent, gate_weight, up_weight, down_weight):
    rows = lax.all_gather(normed, "node", axis=0, tiled=True)
    cots = lax.all_gather(cotangent, "node", axis=0, tiled=True)
    gate_pre = dot(rows, gate_weight, NN)
    up_pre = dot(rows, up_weight, NN)
    sigma = jax.nn.sigmoid(gate_pre)
    activated = gate_pre * sigma
    hidden = (activated * up_pre).astype(BF)
    grad_hidden = dot(cots, down_weight, NT)
    grad_gate = (grad_hidden * up_pre * sigma * (1.0 + gate_pre * (1.0 - sigma))).astype(BF)
    grad_up = (grad_hidden * activated).astype(BF)
    grad_normed = lax.psum_scatter(
        dot(grad_gate, gate_weight, NT) + dot(grad_up, up_weight, NT),
        "node",
        scatter_dimension=0,
        tiled=True,
    ).astype(BF)
    stacked = jnp.concatenate(
        [dot(rows, grad_gate, TN), dot(rows, grad_up, TN), dot(cots, hidden, TN)], axis=0
    )
    weight_grads = lax.psum_scatter(
        stacked.astype(BF), "dp", scatter_dimension=0, tiled=True
    ).astype(F32)
    return grad_normed, weight_grads


def far_kernel(n_dp, normed, cotangent, *far):
    unit = normed.shape[1] // n_dp
    for step, out in enumerate(far, 1):
        owner = lax.axis_index("dp") ^ step
        for j in range(3):
            index = 3 * owner + j
            columns = pl.ds(pl.multiple_of(lax.rem(index, n_dp) * unit, unit), unit)
            out[:, j * unit : (j + 1) * unit] = jnp.where(
                index >= 2 * n_dp, cotangent[:, columns], normed[:, columns]
            )


def load_kernel(first, weight, after, out, token, sem):
    copy = pltpu.make_async_copy(weight.at[pl.ds(first, out.shape[0])], out, sem)
    copy.start()
    token[...] = jnp.zeros(token.shape, token.dtype)
    copy.wait()


def load_rows(weight, first, count, after, name):
    return pl.pallas_call(
        lambda *refs: load_kernel(first, *refs),
        out_shape=(
            pltpu.VMEM((count, weight.shape[1]), weight.dtype),
            jax.ShapeDtypeStruct((8, 128), F32),
        ),
        in_specs=[HBM_SPEC, ANY_SPEC],
        out_specs=(VMEM_SPEC, VMEM_SPEC),
        scratch_shapes=[pltpu.SemaphoreType.DMA],
        compiler_params=pltpu.CompilerParams(vmem_limit_bytes=1 << 20),
        cost_estimate=pl.CostEstimate(
            flops=0, bytes_accessed=2 * count * weight.shape[1], transcendentals=0
        ),
        name=name,
    )(weight, after)


def join_kernel(*refs):
    *pieces, after, out = refs
    start = 0
    for piece in pieces:
        out[:, start : start + piece.shape[1]] = piece[...]
        start += piece.shape[1]


def stack_kernel(*refs):
    *pieces, after, out = refs
    for slot, piece in enumerate(pieces):
        out[slot] = piece[...]


def glue(kernel, shape, pieces, after, name):
    return pl.pallas_call(
        kernel,
        out_shape=jax.ShapeDtypeStruct(shape, BF),
        in_specs=[VMEM_SPEC] * len(pieces) + [ANY_SPEC],
        out_specs=VMEM_SPEC,
        compiler_params=pltpu.CompilerParams(vmem_limit_bytes=4 << 20),
        cost_estimate=pl.CostEstimate(flops=0, bytes_accessed=1 << 18, transcendentals=0),
        name=name,
    )(*pieces, after)


def arrange_kernel(plane, other, after, tokens, far, wide):
    own = plane.shape[1]
    group, width = tokens.shape[1:]
    block = far.shape[1]
    for slot in range(plane.shape[0]):
        for half, source in enumerate((plane, other)):
            start = (half * plane.shape[0] + slot) * own
            wide[start : start + own] = source[slot].astype(F32)
    for i in range(2):
        tokens[i] = wide[:, i * width : (i + 1) * width].astype(BF)
    for i in range(far.shape[0] // group):
        start = 2 * width + i * block
        far[i * group : (i + 1) * group] = wide[:, start : start + block].astype(BF)


def forward_kernel(n_dp, chunk, tokens, gate_a, gate_b, up_a, up, down, *refs):
    *packs, grads_out, up_b, _, _, _, gate_pre, up_pre, grads, down_rows, up_sem, down_sem = refs
    half = gate_a.shape[0]
    columns = gate_a.shape[1]
    up_copy = pltpu.make_async_copy(up.at[pl.ds(half, half)], up_b, up_sem)
    up_copy.start()
    parts = [slice(start, start + chunk) for start in range(0, columns, chunk)]
    down_copies = [
        pltpu.make_async_copy(
            down.at[pl.ds(part.start, chunk)], down_rows.at[pl.ds(part.start, chunk)], down_sem.at[i]
        )
        for i, part in enumerate(parts)
    ]
    for copy in down_copies:
        copy.start()
    for part in parts:
        gate_pre[:, part] = dot(tokens[0, :, :half], gate_a[:, part], NN) + dot(
            tokens[0, :, half:], gate_b[:, part], NN
        )
        up_pre[:, part] = dot(tokens[0, :, :half], up_a[:, part], NN)
    up_copy.wait()
    for part in parts:
        up_pre[:, part] += dot(tokens[0, :, half:], up_b[:, part], NN)
    for part, copy in zip(parts, down_copies):
        copy.wait()
        grad_hidden = dot(tokens[1], down_rows[part, :], NT)
        gate_part = gate_pre[:, part]
        up_part = up_pre[:, part]
        sigma = jax.nn.sigmoid(gate_part)
        activated = gate_part * sigma
        grads[0, :, part] = (
            grad_hidden * up_part * sigma * (1.0 + gate_part * (1.0 - sigma))
        ).astype(BF)
        grads[1, :, part] = (grad_hidden * activated).astype(BF)
        grads[2, :, part] = (activated * up_part).astype(BF)
    grads_out[...] = grads[:2]
    for step, pack in enumerate(packs):
        owner = lax.axis_index("dp") ^ step
        pack[0] = grads[lax.div(3 * owner, n_dp)]
        pack[1] = grads[lax.div(3 * owner + 2, n_dp)]


def backward_kernel(chunk, grads, gate_a, gate_b, up_a, up_b, keep, send):
    half = gate_a.shape[0]
    rows = keep.shape[0]
    for gate, up, base in ((gate_a, up_a, 0), (gate_b, up_b, half)):
        for start in range(0, half, chunk):
            part = slice(start, start + chunk)
            total = dot(grads[0], gate[part, :], NT) + dot(grads[1], up[part, :], NT)
            keep[:, base + start : base + start + chunk] = total[:rows]
            send[:, base + start : base + start + chunk] = total[rows:].astype(BF)


def product_kernel(n_dp, pieces, tokens, far, *refs):
    *packs, out, token, columns, grads, result, sem = refs
    group = tokens.shape[1]
    unit = tokens.shape[2] // n_dp
    d = lax.axis_index("dp")
    token[...] = jnp.zeros(token.shape, token.dtype)
    for slot, pack in enumerate(packs):
        for m in range(2):
            grads[m, slot * group : (slot + 1) * group] = pack[m]
    for j in range(3):
        index = 3 * d + j
        source = pl.ds(pl.multiple_of(lax.rem(index, n_dp) * unit, unit), unit)
        part = slice(j * unit, (j + 1) * unit)
        columns[:group, part] = jnp.where(
            index >= 2 * n_dp, tokens[1, :, source], tokens[0, :, source]
        )
    columns[group:] = far[...]
    copies = []
    for i, (start, count) in enumerate(pieces):
        j = start // unit
        which = lax.div(3 * d + j, n_dp) - lax.div(3 * d, n_dp)
        part = slice(start, start + count)
        result[part] = dot(columns[:, part], grads[which], TN)
        copy = pltpu.make_async_copy(
            result.at[pl.ds(start, count)], out.at[pl.ds(start, count)], sem.at[i]
        )
        copy.start()
        copies.append(copy)
    for copy in copies:
        copy.wait()


def hold_kernel(piece, *refs):
    refs[-1][...] = piece[...]


def final_kernel(own, chip, first, second, third, after, out):
    total = chip[:own]
    for piece in (first, second, third):
        total = total + piece[...].astype(F32)
    out[...] = total.astype(BF)


def shards_group(mesh_shape, normed, cotangent, gate_weight, up_weight, down_weight):
    n_dp, n_node = mesh_shape
    own, width = normed.shape
    hidden = gate_weight.shape[1]
    group = own * n_node
    block = 3 * width // n_dp
    half = width // 2
    chips = range(2, n_node, 2)
    groups = range(1, n_dp)
    weight_bytes = 2 * width * hidden

    def permute(array, axis, step):
        return lax.ppermute(array, axis, xor_pairs(mesh_shape[axis == "node"], step))

    far = pl.pallas_call(
        lambda *refs: far_kernel(n_dp, *refs),
        out_shape=[jax.ShapeDtypeStruct((own, block), BF) for s in groups],
        in_specs=[VMEM_SPEC] * 2,
        out_specs=[VMEM_SPEC] * len(groups),
        compiler_params=pltpu.CompilerParams(vmem_limit_bytes=1 << 20),
        name="far_columns",
    )(normed, cotangent)
    far = [permute(piece, "dp", s) for s, piece in zip(groups, far)]
    gate_hbm, up_hbm, down_hbm = (in_hbm(w) for w in (gate_weight, up_weight, down_weight))
    gate_a, token = load_rows(gate_hbm, 0, half, normed, "load_gate_a")
    tall = 2 * width + len(groups) * block
    mine = glue(join_kernel, (own, tall), [normed, cotangent, *far], token, "join")
    plane = [mine] + [permute(mine, "node", s) for s in chips]
    gate_b, token = load_rows(gate_hbm, half, half, token, "load_gate_b")
    plane = glue(stack_kernel, (len(plane), own, tall), plane, token, "stack")
    other = permute(plane, "node", 1)
    up_a, token = load_rows(up_hbm, 0, half, token, "load_up_a")
    tokens, far = pl.pallas_call(
        arrange_kernel,
        out_shape=(
            jax.ShapeDtypeStruct((2, group, width), BF),
            jax.ShapeDtypeStruct(((n_dp - 1) * group, block), BF),
        ),
        in_specs=[VMEM_SPEC] * 2 + [ANY_SPEC],
        out_specs=(VMEM_SPEC, VMEM_SPEC),
        scratch_shapes=[pltpu.VMEM((group, tall), F32)],
        compiler_params=pltpu.CompilerParams(vmem_limit_bytes=4 << 20),
        cost_estimate=pl.CostEstimate(flops=0, bytes_accessed=1 << 20, transcendentals=0),
        name="arrange",
    )(plane, other, token)

    pack = jax.ShapeDtypeStruct((2, group, hidden), BF)
    chunk = 256
    *packs, grads, up_b, gate_a, gate_b, up_a = pl.pallas_call(
        lambda *refs: forward_kernel(n_dp, chunk, *refs),
        out_shape=[pack] * (n_dp + 1) + [pltpu.VMEM((half, hidden), BF)] * 4,
        in_specs=[VMEM_SPEC] * 4 + [HBM_SPEC] * 2,
        out_specs=[VMEM_SPEC] * (n_dp + 5),
        input_output_aliases={1: n_dp + 2, 2: n_dp + 3, 3: n_dp + 4},
        scratch_shapes=[
            pltpu.VMEM((group, hidden), F32),
            pltpu.VMEM((group, hidden), F32),
            pltpu.VMEM((3, group, hidden), BF),
            pltpu.VMEM((hidden, width), BF),
            pltpu.SemaphoreType.DMA,
            pltpu.SemaphoreType.DMA((hidden // chunk,)),
        ],
        compiler_params=pltpu.CompilerParams(vmem_limit_bytes=20 << 20),
        cost_estimate=pl.CostEstimate(
            flops=6 * group * width * hidden, bytes_accessed=2 * weight_bytes, transcendentals=0
        ),
        name="forward",
    )(tokens, in_vmem(gate_a), in_vmem(gate_b), in_vmem(up_a), up_hbm, down_hbm)

    packs = [packs[0]] + [permute(packs[s], "dp", s) for s in groups]

    keep, send = pl.pallas_call(
        lambda *refs: backward_kernel(chunk, *refs),
        out_shape=(
            jax.ShapeDtypeStruct((group // 2, width), F32),
            jax.ShapeDtypeStruct((group // 2, width), BF),
        ),
        in_specs=[VMEM_SPEC] * 5,
        out_specs=(VMEM_SPEC, VMEM_SPEC),
        compiler_params=pltpu.CompilerParams(vmem_limit_bytes=4 << 20),
        cost_estimate=pl.CostEstimate(
            flops=4 * group * width * hidden, bytes_accessed=2 * weight_bytes, transcendentals=0
        ),
        name="backward",
    )(grads, in_vmem(gate_a), in_vmem(gate_b), in_vmem(up_a), in_vmem(up_b))

    send = pl.pallas_call(
        hold_kernel,
        out_shape=jax.ShapeDtypeStruct(send.shape, BF),
        in_specs=[VMEM_SPEC] + [ANY_SPEC] * (n_dp - 1),
        out_specs=VMEM_SPEC,
        compiler_params=pltpu.CompilerParams(vmem_limit_bytes=1 << 20),
        name="hold",
    )(send, *packs[1:])
    chip = keep + permute(send, "node", 1).astype(F32)
    pieces = [
        permute(chip[own * slot : own * (slot + 1)].astype(BF), "node", s)
        for slot, s in enumerate(chips, 1)
    ]

    cuts = [(start, 256) for start in range(0, block, 256)]
    weight_grads, token = pl.pallas_call(
        lambda *refs: product_kernel(n_dp, cuts, *refs),
        out_shape=(
            pltpu.HBM((block, hidden), F32),
            jax.ShapeDtypeStruct((8, 128), F32),
        ),
        in_specs=[VMEM_SPEC] * (n_dp + 2),
        out_specs=(HBM_SPEC, VMEM_SPEC),
        scratch_shapes=[
            pltpu.VMEM((n_dp * group, block), BF),
            pltpu.VMEM((2, n_dp * group, hidden), BF),
            pltpu.VMEM((block, hidden), F32),
            pltpu.SemaphoreType.DMA((len(cuts),)),
        ],
        compiler_params=pltpu.CompilerParams(vmem_limit_bytes=32 << 20),
        cost_estimate=pl.CostEstimate(
            flops=2 * n_dp * group * block * hidden,
            bytes_accessed=4 * block * hidden,
            transcendentals=0,
        ),
        name="product",
    )(tokens, far, *packs)
    grad_normed = pl.pallas_call(
        lambda *refs: final_kernel(own, *refs),
        out_shape=jax.ShapeDtypeStruct((own, width), BF),
        in_specs=[VMEM_SPEC] * 4 + [ANY_SPEC],
        out_specs=VMEM_SPEC,
        compiler_params=pltpu.CompilerParams(vmem_limit_bytes=2 << 20),
        name="final_sum",
    )(chip, *pieces, token)
    return grad_normed, weight_grads


def solution(mesh):
    n_dp, n_node = mesh.shape["dp"], mesh.shape["node"]

    def shards(*arrays):
        normed, gate_weight = arrays[0], arrays[2]
        rows, width = normed.shape
        hidden = gate_weight.shape[1]
        fits = (
            n_dp == 4
            and n_node == 8
            and rows * n_node == 16
            and hidden % 256 == 0
            and hidden * width * 6 <= 46 << 20
            and width % (n_dp * 256) == 0
        )
        if fits:
            return shards_group((n_dp, n_node), *arrays)
        return shards_any(n_dp, *arrays)

    in_specs = (
        P(("dp", "node"), None),
        P(("dp", "node"), None),
        P(None, "node"),
        P(None, "node"),
        P("node", None),
    )
    out_specs = (P(("dp", "node"), None), P("dp", "node"))
    return jax.shard_map(shards, mesh=mesh, in_specs=in_specs, out_specs=out_specs, check_vma=False)
```

```python
import jax
import jax.numpy as jnp
from jax import lax
from jax.experimental import pallas as pl
from jax.experimental.pallas import tpu as pltpu
from jax.sharding import PartitionSpec as P

BF = jnp.bfloat16
F32 = jnp.float32
NN = (((1,), (0,)), ((), ()))
NT = (((1,), (1,)), ((), ()))
TN = (((0,), (0,)), ((), ()))
ANY_SPEC = pl.BlockSpec(memory_space=pl.ANY)
HBM_SPEC = pl.BlockSpec(memory_space=pltpu.HBM)
VMEM_SPEC = pl.BlockSpec(memory_space=pltpu.VMEM)


def dot(left, right, dims):
    return lax.dot_general(left, right, dims, preferred_element_type=F32)


def in_hbm(array):
    return pltpu.with_memory_space_constraint(array, pltpu.HBM)


def in_vmem(array):
    return pltpu.with_memory_space_constraint(array, pltpu.VMEM)


def xor_pairs(count, step):
    return [(i, i ^ step) for i in range(count)]


def shards_any(n_dp, normed, cotangent, gate_weight, up_weight, down_weight):
    rows = lax.all_gather(normed, "node", axis=0, tiled=True)
    cots = lax.all_gather(cotangent, "node", axis=0, tiled=True)
    gate_pre = dot(rows, gate_weight, NN)
    up_pre = dot(rows, up_weight, NN)
    sigma = jax.nn.sigmoid(gate_pre)
    activated = gate_pre * sigma
    hidden = (activated * up_pre).astype(BF)
    grad_hidden = dot(cots, down_weight, NT)
    grad_gate = (grad_hidden * up_pre * sigma * (1.0 + gate_pre * (1.0 - sigma))).astype(BF)
    grad_up = (grad_hidden * activated).astype(BF)
    grad_normed = lax.psum_scatter(
        dot(grad_gate, gate_weight, NT) + dot(grad_up, up_weight, NT),
        "node",
        scatter_dimension=0,
        tiled=True,
    ).astype(BF)
    stacked = jnp.concatenate(
        [dot(rows, grad_gate, TN), dot(rows, grad_up, TN), dot(cots, hidden, TN)], axis=0
    )
    weight_grads = lax.psum_scatter(
        stacked.astype(BF), "dp", scatter_dimension=0, tiled=True
    ).astype(F32)
    return grad_normed, weight_grads


def join_kernel(normed, cotangent, out, sem):
    copies = [
        pltpu.make_async_copy(source, out.at[i], sem.at[i])
        for i, source in enumerate((normed, cotangent))
    ]
    for copy in copies:
        copy.start()
    for copy in copies:
        copy.wait()


def load_kernel(first, weight, after, out, token, sem):
    copy = pltpu.make_async_copy(weight.at[pl.ds(first, out.shape[0])], out, sem)
    copy.start()
    token[...] = jnp.zeros(token.shape, token.dtype)
    copy.wait()


def load_rows(weight, first, count, after, name):
    return pl.pallas_call(
        lambda *refs: load_kernel(first, *refs),
        out_shape=(
            pltpu.VMEM((count, weight.shape[1]), weight.dtype),
            jax.ShapeDtypeStruct((8, 128), F32),
        ),
        in_specs=[HBM_SPEC, ANY_SPEC],
        out_specs=(VMEM_SPEC, VMEM_SPEC),
        scratch_shapes=[pltpu.SemaphoreType.DMA],
        compiler_params=pltpu.CompilerParams(vmem_limit_bytes=1 << 20),
        cost_estimate=pl.CostEstimate(
            flops=0, bytes_accessed=2 * count * weight.shape[1], transcendentals=0
        ),
        name=name,
    )(weight, after)


def stack_kernel(*refs):
    *pieces, after, out = refs
    for slot, piece in enumerate(pieces):
        out[slot] = piece[...]


def glue(kernel, shape, pieces, after, name):
    return pl.pallas_call(
        kernel,
        out_shape=jax.ShapeDtypeStruct(shape, BF),
        in_specs=[VMEM_SPEC] * len(pieces) + [ANY_SPEC],
        out_specs=VMEM_SPEC,
        compiler_params=pltpu.CompilerParams(vmem_limit_bytes=4 << 20),
        cost_estimate=pl.CostEstimate(flops=0, bytes_accessed=1 << 18, transcendentals=0),
        name=name,
    )(*pieces, after)


def arrange_kernel(n_dp, plane, other, after, tokens, *refs):
    *columns, wide = refs
    own = plane.shape[2]
    unit = tokens.shape[2] // n_dp
    for i in range(2):
        for slot in range(plane.shape[0]):
            for half, source in enumerate((plane, other)):
                start = (half * plane.shape[0] + slot) * own
                wide[i, start : start + own] = source[slot, i].astype(F32)
        tokens[i] = wide[i].astype(BF)
    for step, out in enumerate(columns):
        owner = lax.axis_index("dp") ^ step
        for j in range(3):
            index = 3 * owner + j
            part = pl.ds(pl.multiple_of(lax.rem(index, n_dp) * unit, unit), unit)
            out[:, j * unit : (j + 1) * unit] = tokens[lax.div(index, 2 * n_dp), :, part]


def forward_kernel(chunk, tokens, gate_a, gate_b, down, up_hbm, grads, up, _a, _b, gate_pre, grad_hidden, sem):
    half, columns = gate_a.shape
    parts = [slice(start, start + chunk) for start in range(0, columns, chunk)]
    copies = [
        pltpu.make_async_copy(
            up_hbm.at[pl.ds(i * half, half)], up.at[pl.ds(i * half, half)], sem.at[i]
        )
        for i in range(2)
    ]
    for copy in copies:
        copy.start()
    for part in parts:
        gate_pre[:, part] = dot(tokens[0, :, :half], gate_a[:, part], NN) + dot(
            tokens[0, :, half:], gate_b[:, part], NN
        )
    for part in parts:
        grad_hidden[:, part] = dot(tokens[1], down[part, :], NT)
    for copy in copies:
        copy.wait()
    for part in parts:
        up_part = dot(tokens[0], up[:, part], NN)
        gate_part = gate_pre[:, part]
        sigma = jax.nn.sigmoid(gate_part)
        activated = gate_part * sigma
        grads[0, :, part] = (
            grad_hidden[:, part] * up_part * sigma * (1.0 + gate_part * (1.0 - sigma))
        ).astype(BF)
        grads[1, :, part] = (grad_hidden[:, part] * activated).astype(BF)
        grads[2, :, part] = (activated * up_part).astype(BF)


def pack_kernel(n_dp, grads, *refs):
    for step, pack in enumerate(refs[-n_dp:]):
        owner = lax.axis_index("dp") ^ step
        pack[0] = grads[lax.div(3 * owner, n_dp)]
        pack[1] = grads[lax.div(3 * owner + 2, n_dp)]


def backward_kernel(chunk, grads, gate_a, gate_b, up_all, keep, send):
    half = gate_a.shape[0]
    rows = keep.shape[0]
    for gate, base in ((gate_a, 0), (gate_b, half)):
        for start in range(0, half, chunk):
            part = slice(start, start + chunk)
            total = dot(grads[0], gate[part, :], NT) + dot(
                grads[1], up_all[base + start : base + start + chunk, :], NT
            )
            keep[:, base + start : base + start + chunk] = total[:rows]
            send[:, base + start : base + start + chunk] = total[rows:].astype(BF)


def product_kernel(n_dp, pieces, *refs):
    sources, packs = refs[:n_dp], refs[n_dp : 2 * n_dp]
    out, token, columns, grads, result, sem = refs[2 * n_dp :]
    group, block = sources[0].shape
    unit = block // 3
    d = lax.axis_index("dp")
    token[...] = jnp.zeros(token.shape, token.dtype)
    for slot in range(n_dp):
        rows = slice(slot * group, (slot + 1) * group)
        columns[rows] = sources[slot][...]
        for m in range(2):
            grads[m, rows] = packs[slot][m]
    copies = []
    for i, (start, count) in enumerate(pieces):
        j = start // unit
        which = lax.div(3 * d + j, n_dp) - lax.div(3 * d, n_dp)
        part = slice(start, start + count)
        result[part] = dot(columns[:, part], grads[which], TN)
        copy = pltpu.make_async_copy(
            result.at[pl.ds(start, count)], out.at[pl.ds(start, count)], sem.at[i]
        )
        copy.start()
        copies.append(copy)
    for copy in copies:
        copy.wait()


def hold_kernel(piece, *refs):
    refs[-1][...] = piece[...]


def final_kernel(own, chip, first, second, third, after, out):
    total = chip[:own]
    for piece in (first, second, third):
        total = total + piece[...].astype(F32)
    out[...] = total.astype(BF)


def shards_group(mesh_shape, normed, cotangent, gate_weight, up_weight, down_weight):
    n_dp, n_node = mesh_shape
    own, width = normed.shape
    hidden = gate_weight.shape[1]
    group = own * n_node
    block = 3 * width // n_dp
    half = width // 2
    chips = range(2, n_node, 2)
    groups = range(1, n_dp)
    weight_bytes = 2 * width * hidden

    def permute(array, axis, step):
        return lax.ppermute(array, axis, xor_pairs(mesh_shape[axis == "node"], step))

    mine = pl.pallas_call(
        join_kernel,
        out_shape=jax.ShapeDtypeStruct((2, own, width), BF),
        in_specs=[HBM_SPEC] * 2,
        out_specs=VMEM_SPEC,
        scratch_shapes=[pltpu.SemaphoreType.DMA((2,))],
        compiler_params=pltpu.CompilerParams(vmem_limit_bytes=1 << 20),
        name="join",
    )(in_hbm(normed), in_hbm(cotangent))
    gate_hbm, up_hbm = in_hbm(gate_weight), in_hbm(up_weight)
    plane = [mine] + [permute(mine, "node", s) for s in chips]
    gate_a, token = load_rows(gate_hbm, 0, half, in_hbm(normed), "load_gate_a")
    plane = glue(stack_kernel, (len(plane), 2, own, width), plane, token, "stack")
    other = permute(plane, "node", 1)
    gate_b, token = load_rows(gate_hbm, half, half, token, "load_gate_b")
    piece = jax.ShapeDtypeStruct((group, block), BF)
    tokens, *columns = pl.pallas_call(
        lambda *refs: arrange_kernel(n_dp, *refs),
        out_shape=[jax.ShapeDtypeStruct((2, group, width), BF)] + [piece] * n_dp,
        in_specs=[VMEM_SPEC] * 2 + [ANY_SPEC],
        out_specs=[VMEM_SPEC] * (n_dp + 1),
        scratch_shapes=[pltpu.VMEM((2, group, width), F32)],
        compiler_params=pltpu.CompilerParams(vmem_limit_bytes=4 << 20),
        cost_estimate=pl.CostEstimate(flops=0, bytes_accessed=1 << 20, transcendentals=0),
        name="arrange",
    )(plane, other, token)
    columns = [columns[0]] + [permute(columns[s], "dp", s) for s in groups]

    chunk = 256
    grads, up, gate_a, gate_b = pl.pallas_call(
        lambda *refs: forward_kernel(chunk, *refs),
        out_shape=[
            jax.ShapeDtypeStruct((3, group, hidden), BF),
            pltpu.VMEM((width, hidden), BF),
            pltpu.VMEM((half, hidden), BF),
            pltpu.VMEM((half, hidden), BF),
        ],
        in_specs=[VMEM_SPEC] * 4 + [HBM_SPEC],
        out_specs=[VMEM_SPEC] * 4,
        input_output_aliases={1: 2, 2: 3},
        scratch_shapes=[
            pltpu.VMEM((group, hidden), F32),
            pltpu.VMEM((group, hidden), F32),
            pltpu.SemaphoreType.DMA((2,)),
        ],
        compiler_params=pltpu.CompilerParams(vmem_limit_bytes=4 << 20),
        cost_estimate=pl.CostEstimate(
            flops=6 * group * width * hidden, bytes_accessed=2 * weight_bytes, transcendentals=0
        ),
        name="forward",
    )(tokens, in_vmem(gate_a), in_vmem(gate_b), in_vmem(down_weight), up_hbm)

    packs = pl.pallas_call(
        lambda *refs: pack_kernel(n_dp, *refs),
        out_shape=[jax.ShapeDtypeStruct((2, group, hidden), BF)] * n_dp,
        in_specs=[VMEM_SPEC] + [ANY_SPEC] * (n_dp - 1),
        out_specs=[VMEM_SPEC] * n_dp,
        compiler_params=pltpu.CompilerParams(vmem_limit_bytes=1 << 20),
        name="pack",
    )(grads, *columns[1:])
    packs = [packs[0]] + [permute(packs[s], "dp", s) for s in groups]

    keep, send = pl.pallas_call(
        lambda *refs: backward_kernel(chunk, *refs),
        out_shape=(
            jax.ShapeDtypeStruct((group // 2, width), F32),
            jax.ShapeDtypeStruct((group // 2, width), BF),
        ),
        in_specs=[VMEM_SPEC] * 4,
        out_specs=(VMEM_SPEC, VMEM_SPEC),
        compiler_params=pltpu.CompilerParams(vmem_limit_bytes=4 << 20),
        cost_estimate=pl.CostEstimate(
            flops=4 * group * width * hidden, bytes_accessed=2 * weight_bytes, transcendentals=0
        ),
        name="backward",
    )(grads, in_vmem(gate_a), in_vmem(gate_b), in_vmem(up))

    send = pl.pallas_call(
        hold_kernel,
        out_shape=jax.ShapeDtypeStruct(send.shape, BF),
        in_specs=[VMEM_SPEC] + [ANY_SPEC] * (n_dp - 1),
        out_specs=VMEM_SPEC,
        compiler_params=pltpu.CompilerParams(vmem_limit_bytes=1 << 20),
        name="hold",
    )(send, *packs[1:])
    chip = keep + permute(send, "node", 1).astype(F32)
    pieces = [
        permute(chip[own * slot : own * (slot + 1)].astype(BF), "node", s)
        for slot, s in enumerate(chips, 1)
    ]

    cuts = [(start, 256) for start in range(0, block, 256)]
    weight_grads, token = pl.pallas_call(
        lambda *refs: product_kernel(n_dp, cuts, *refs),
        out_shape=(
            pltpu.HBM((block, hidden), F32),
            jax.ShapeDtypeStruct((8, 128), F32),
        ),
        in_specs=[VMEM_SPEC] * (2 * n_dp),
        out_specs=(HBM_SPEC, VMEM_SPEC),
        scratch_shapes=[
            pltpu.VMEM((n_dp * group, block), BF),
            pltpu.VMEM((2, n_dp * group, hidden), BF),
            pltpu.VMEM((block, hidden), F32),
            pltpu.SemaphoreType.DMA((len(cuts),)),
        ],
        compiler_params=pltpu.CompilerParams(vmem_limit_bytes=32 << 20),
        cost_estimate=pl.CostEstimate(
            flops=2 * n_dp * group * block * hidden,
            bytes_accessed=4 * block * hidden,
            transcendentals=0,
        ),
        name="product",
    )(*columns, *packs)
    grad_normed = pl.pallas_call(
        lambda *refs: final_kernel(own, *refs),
        out_shape=jax.ShapeDtypeStruct((own, width), BF),
        in_specs=[VMEM_SPEC] * 4 + [ANY_SPEC],
        out_specs=VMEM_SPEC,
        compiler_params=pltpu.CompilerParams(vmem_limit_bytes=2 << 20),
        name="final_sum",
    )(chip, *pieces, token)
    return grad_normed, weight_grads


def solution(mesh):
    n_dp, n_node = mesh.shape["dp"], mesh.shape["node"]

    def shards(*arrays):
        normed, gate_weight = arrays[0], arrays[2]
        rows, width = normed.shape
        hidden = gate_weight.shape[1]
        fits = (
            n_dp == 4
            and n_node == 8
            and rows * n_node == 16
            and hidden % 256 == 0
            and hidden * width * 6 <= 46 << 20
            and width % (n_dp * 256) == 0
        )
        if fits:
            return shards_group((n_dp, n_node), *arrays)
        return shards_any(n_dp, *arrays)

    in_specs = (
        P(("dp", "node"), None),
        P(("dp", "node"), None),
        P(None, "node"),
        P(None, "node"),
        P("node", None),
    )
    out_specs = (P(("dp", "node"), None), P("dp", "node"))
    return jax.shard_map(shards, mesh=mesh, in_specs=in_specs, out_specs=out_specs, check_vma=False)
```

```python
import jax
import jax.numpy as jnp
from jax import lax
from jax.experimental import pallas as pl
from jax.experimental.pallas import tpu as pltpu
from jax.sharding import PartitionSpec as P

BF = jnp.bfloat16
F32 = jnp.float32
NN = (((1,), (0,)), ((), ()))
NT = (((1,), (1,)), ((), ()))
TN = (((0,), (0,)), ((), ()))
ANY_SPEC = pl.BlockSpec(memory_space=pl.ANY)
HBM_SPEC = pl.BlockSpec(memory_space=pltpu.HBM)
VMEM_SPEC = pl.BlockSpec(memory_space=pltpu.VMEM)


def dot(left, right, dims):
    return lax.dot_general(left, right, dims, preferred_element_type=F32)


def in_hbm(array):
    return pltpu.with_memory_space_constraint(array, pltpu.HBM)


def in_vmem(array):
    return pltpu.with_memory_space_constraint(array, pltpu.VMEM)


def xor_pairs(count, step):
    return [(i, i ^ step) for i in range(count)]


def shards_any(n_dp, normed, cotangent, gate_weight, up_weight, down_weight):
    rows = lax.all_gather(normed, "node", axis=0, tiled=True)
    cots = lax.all_gather(cotangent, "node", axis=0, tiled=True)
    gate_pre = dot(rows, gate_weight, NN)
    up_pre = dot(rows, up_weight, NN)
    sigma = jax.nn.sigmoid(gate_pre)
    activated = gate_pre * sigma
    hidden = (activated * up_pre).astype(BF)
    grad_hidden = dot(cots, down_weight, NT)
    grad_gate = (grad_hidden * up_pre * sigma * (1.0 + gate_pre * (1.0 - sigma))).astype(BF)
    grad_up = (grad_hidden * activated).astype(BF)
    grad_normed = lax.psum_scatter(
        dot(grad_gate, gate_weight, NT) + dot(grad_up, up_weight, NT),
        "node",
        scatter_dimension=0,
        tiled=True,
    ).astype(BF)
    stacked = jnp.concatenate(
        [dot(rows, grad_gate, TN), dot(rows, grad_up, TN), dot(cots, hidden, TN)], axis=0
    )
    weight_grads = lax.psum_scatter(
        stacked.astype(BF), "dp", scatter_dimension=0, tiled=True
    ).astype(F32)
    return grad_normed, weight_grads


def join_kernel(normed, cotangent, out, sem):
    copies = [
        pltpu.make_async_copy(source, out.at[i], sem.at[i])
        for i, source in enumerate((normed, cotangent))
    ]
    for copy in copies:
        copy.start()
    for copy in copies:
        copy.wait()


def load_kernel(first, count, weight, after, *refs):
    out, token, sem = refs[-3:]
    part = pl.ds(first, count)
    copy = pltpu.make_async_copy(weight.at[part], out.at[part], sem)
    copy.start()
    token[...] = jnp.zeros(token.shape, token.dtype)
    copy.wait()


def load_rows(weight, first, count, after, held, name):
    return pl.pallas_call(
        lambda *refs: load_kernel(first, count, *refs),
        out_shape=(
            pltpu.VMEM(weight.shape, weight.dtype),
            jax.ShapeDtypeStruct((8, 128), F32),
        ),
        in_specs=[HBM_SPEC, ANY_SPEC] + [VMEM_SPEC] * len(held),
        out_specs=(VMEM_SPEC, VMEM_SPEC),
        input_output_aliases={2: 0} if held else {},
        scratch_shapes=[pltpu.SemaphoreType.DMA],
        compiler_params=pltpu.CompilerParams(vmem_limit_bytes=1 << 20),
        cost_estimate=pl.CostEstimate(
            flops=0, bytes_accessed=2 * count * weight.shape[1], transcendentals=0
        ),
        name=name,
    )(weight, after, *held)


def stack_kernel(*refs):
    *pieces, after, out = refs
    for slot, piece in enumerate(pieces):
        out[slot] = piece[...]


def glue(kernel, shape, pieces, after, name):
    return pl.pallas_call(
        kernel,
        out_shape=jax.ShapeDtypeStruct(shape, BF),
        in_specs=[VMEM_SPEC] * len(pieces) + [ANY_SPEC],
        out_specs=VMEM_SPEC,
        compiler_params=pltpu.CompilerParams(vmem_limit_bytes=4 << 20),
        cost_estimate=pl.CostEstimate(flops=0, bytes_accessed=1 << 18, transcendentals=0),
        name=name,
    )(*pieces, after)


def arrange_kernel(n_dp, chips, *refs):
    sources, (tokens, *columns, wide) = refs[:chips], refs[chips + 1 :]
    own = sources[0].shape[2]
    unit = tokens.shape[2] // n_dp
    for i in range(2):
        for slot, source in enumerate(sources):
            for core in range(2):
                start = (core * chips + slot) * own
                wide[i, start : start + own] = source[core, i].astype(F32)
        tokens[i] = wide[i].astype(BF)
    for step, out in enumerate(columns):
        owner = lax.axis_index("dp") ^ step
        for j in range(3):
            index = 3 * owner + j
            part = pl.ds(pl.multiple_of(lax.rem(index, n_dp) * unit, unit), unit)
            out[:, j * unit : (j + 1) * unit] = tokens[lax.div(index, 2 * n_dp), :, part]


def forward_kernel(chunk, tokens, gate, down, up_hbm, grads, up, _, gate_pre, grad_hidden, sem):
    rows, columns = gate.shape
    parts = [slice(start, start + chunk) for start in range(0, columns, chunk)]
    piece = rows // sem.shape[0]
    copies = [
        pltpu.make_async_copy(
            up_hbm.at[pl.ds(i * piece, piece)], up.at[pl.ds(i * piece, piece)], sem.at[i]
        )
        for i in range(sem.shape[0])
    ]
    for copy in copies:
        copy.start(priority=1)
    for part in parts:
        gate_pre[:, part] = dot(tokens[0], gate[:, part], NN)
        grad_hidden[:, part] = dot(tokens[1], down[part, :], NT)
    for copy in copies:
        copy.wait()
    for part in parts:
        up_part = dot(tokens[0], up[:, part], NN)
        gate_part = gate_pre[:, part]
        sigma = jax.nn.sigmoid(gate_part)
        activated = gate_part * sigma
        grads[0, :, part] = (
            grad_hidden[:, part] * up_part * sigma * (1.0 + gate_part * (1.0 - sigma))
        ).astype(BF)
        grads[1, :, part] = (grad_hidden[:, part] * activated).astype(BF)
        grads[2, :, part] = (activated * up_part).astype(BF)


def pack_kernel(n_dp, grads, *refs):
    for step, pack in enumerate(refs[-n_dp:]):
        owner = lax.axis_index("dp") ^ step
        pack[0] = grads[lax.div(3 * owner, n_dp)]
        pack[1] = grads[lax.div(3 * owner + 2, n_dp)]


def backward_kernel(chunk, grads, gate, up, keep, send):
    rows = keep.shape[0]
    for start in range(0, gate.shape[0], chunk):
        part = slice(start, start + chunk)
        total = dot(grads[0], gate[part, :], NT) + dot(grads[1], up[part, :], NT)
        keep[:, part] = total[:rows]
        send[:, part] = total[rows:].astype(BF)


def product_kernel(n_dp, pieces, *refs):
    sources, packs = refs[:n_dp], refs[n_dp : 2 * n_dp]
    out, token, columns, grads, result, sem = refs[2 * n_dp :]
    group, block = sources[0].shape
    unit = block // 3
    d = lax.axis_index("dp")
    token[...] = jnp.zeros(token.shape, token.dtype)
    for slot in range(n_dp):
        rows = slice(slot * group, (slot + 1) * group)
        columns[rows] = sources[slot][...]
        for m in range(2):
            grads[m, rows] = packs[slot][m]
    copies = []
    for i, (start, count) in enumerate(pieces):
        j = start // unit
        which = lax.div(3 * d + j, n_dp) - lax.div(3 * d, n_dp)
        part = slice(start, start + count)
        result[part] = dot(columns[:, part], grads[which], TN)
        copy = pltpu.make_async_copy(
            result.at[pl.ds(start, count)], out.at[pl.ds(start, count)], sem.at[i]
        )
        copy.start()
        copies.append(copy)
    for copy in copies:
        copy.wait()


def hold_kernel(piece, *refs):
    refs[-1][...] = piece[...]


def final_kernel(own, chip, first, second, third, after, out):
    total = chip[:own]
    for piece in (first, second, third):
        total = total + piece[...].astype(F32)
    out[...] = total.astype(BF)


def shards_group(mesh_shape, normed, cotangent, gate_weight, up_weight, down_weight):
    n_dp, n_node = mesh_shape
    own, width = normed.shape
    hidden = gate_weight.shape[1]
    group = own * n_node
    block = 3 * width // n_dp
    half, quarter = width // 2, width // 4
    chips = range(2, n_node, 2)
    groups = range(1, n_dp)
    weight_bytes = 2 * width * hidden

    def permute(array, axis, step):
        return lax.ppermute(array, axis, xor_pairs(mesh_shape[axis == "node"], step))

    mine = pl.pallas_call(
        join_kernel,
        out_shape=jax.ShapeDtypeStruct((2, own, width), BF),
        in_specs=[HBM_SPEC] * 2,
        out_specs=VMEM_SPEC,
        scratch_shapes=[pltpu.SemaphoreType.DMA((2,))],
        compiler_params=pltpu.CompilerParams(vmem_limit_bytes=1 << 20),
        name="join",
    )(in_hbm(normed), in_hbm(cotangent))
    gate_hbm, up_hbm = in_hbm(gate_weight), in_hbm(up_weight)
    other = permute(mine, "node", 1)
    gate, token = load_rows(gate_hbm, 0, quarter, in_hbm(normed), (), "load_gate_a")
    pair = glue(stack_kernel, (2, 2, own, width), [mine, other], token, "stack")
    plane = [pair] + [permute(pair, "node", s) for s in chips]
    gate, token = load_rows(
        gate_hbm, quarter, width - quarter, token, (in_vmem(gate),), "load_gate_b"
    )
    piece = jax.ShapeDtypeStruct((group, block), BF)
    tokens, *columns = pl.pallas_call(
        lambda *refs: arrange_kernel(n_dp, len(plane), *refs),
        out_shape=[jax.ShapeDtypeStruct((2, group, width), BF)] + [piece] * n_dp,
        in_specs=[VMEM_SPEC] * len(plane) + [ANY_SPEC],
        out_specs=[VMEM_SPEC] * (n_dp + 1),
        scratch_shapes=[pltpu.VMEM((2, group, width), F32)],
        compiler_params=pltpu.CompilerParams(vmem_limit_bytes=4 << 20),
        cost_estimate=pl.CostEstimate(flops=0, bytes_accessed=1 << 20, transcendentals=0),
        name="arrange",
    )(*plane, token)
    columns = [columns[0]] + [permute(columns[s], "dp", s) for s in groups]

    chunk = 256
    grads, up, gate = pl.pallas_call(
        lambda *refs: forward_kernel(chunk, *refs),
        out_shape=[
            jax.ShapeDtypeStruct((3, group, hidden), BF),
            pltpu.VMEM((width, hidden), BF),
            pltpu.VMEM((width, hidden), BF),
        ],
        in_specs=[VMEM_SPEC] * 3 + [HBM_SPEC],
        out_specs=[VMEM_SPEC] * 3,
        input_output_aliases={1: 2},
        scratch_shapes=[
            pltpu.VMEM((group, hidden), F32),
            pltpu.VMEM((group, hidden), F32),
            pltpu.SemaphoreType.DMA((8,)),
        ],
        compiler_params=pltpu.CompilerParams(vmem_limit_bytes=4 << 20),
        cost_estimate=pl.CostEstimate(
            flops=6 * group * width * hidden, bytes_accessed=2 * weight_bytes, transcendentals=0
        ),
        name="forward",
    )(tokens, in_vmem(gate), in_vmem(down_weight), up_hbm)

    packs = pl.pallas_call(
        lambda *refs: pack_kernel(n_dp, *refs),
        out_shape=[jax.ShapeDtypeStruct((2, group, hidden), BF)] * n_dp,
        in_specs=[VMEM_SPEC] + [ANY_SPEC] * (n_dp - 1),
        out_specs=[VMEM_SPEC] * n_dp,
        compiler_params=pltpu.CompilerParams(vmem_limit_bytes=1 << 20),
        name="pack",
    )(grads, *columns[1:])
    packs = [packs[0]] + [permute(packs[s], "dp", s) for s in groups]

    keep, send = pl.pallas_call(
        lambda *refs: backward_kernel(chunk, *refs),
        out_shape=(
            jax.ShapeDtypeStruct((group // 2, width), F32),
            jax.ShapeDtypeStruct((group // 2, width), BF),
        ),
        in_specs=[VMEM_SPEC] * 3,
        out_specs=(VMEM_SPEC, VMEM_SPEC),
        compiler_params=pltpu.CompilerParams(vmem_limit_bytes=4 << 20),
        cost_estimate=pl.CostEstimate(
            flops=4 * group * width * hidden, bytes_accessed=2 * weight_bytes, transcendentals=0
        ),
        name="backward",
    )(grads, in_vmem(gate), in_vmem(up))

    send = pl.pallas_call(
        hold_kernel,
        out_shape=jax.ShapeDtypeStruct(send.shape, BF),
        in_specs=[VMEM_SPEC] + [ANY_SPEC] * (n_dp - 1),
        out_specs=VMEM_SPEC,
        compiler_params=pltpu.CompilerParams(vmem_limit_bytes=1 << 20),
        name="hold",
    )(send, *packs[1:])
    chip = keep + permute(send, "node", 1).astype(F32)
    pieces = [
        permute(chip[own * slot : own * (slot + 1)].astype(BF), "node", s)
        for slot, s in enumerate(chips, 1)
    ]

    cuts = [(start, 256) for start in range(0, block, 256)]
    weight_grads, token = pl.pallas_call(
        lambda *refs: product_kernel(n_dp, cuts, *refs),
        out_shape=(
            pltpu.HBM((block, hidden), F32),
            jax.ShapeDtypeStruct((8, 128), F32),
        ),
        in_specs=[VMEM_SPEC] * (2 * n_dp),
        out_specs=(HBM_SPEC, VMEM_SPEC),
        scratch_shapes=[
            pltpu.VMEM((n_dp * group, block), BF),
            pltpu.VMEM((2, n_dp * group, hidden), BF),
            pltpu.VMEM((block, hidden), F32),
            pltpu.SemaphoreType.DMA((len(cuts),)),
        ],
        compiler_params=pltpu.CompilerParams(vmem_limit_bytes=32 << 20),
        cost_estimate=pl.CostEstimate(
            flops=2 * n_dp * group * block * hidden,
            bytes_accessed=4 * block * hidden,
            transcendentals=0,
        ),
        name="product",
    )(*columns, *packs)
    grad_normed = pl.pallas_call(
        lambda *refs: final_kernel(own, *refs),
        out_shape=jax.ShapeDtypeStruct((own, width), BF),
        in_specs=[VMEM_SPEC] * 4 + [ANY_SPEC],
        out_specs=VMEM_SPEC,
        compiler_params=pltpu.CompilerParams(vmem_limit_bytes=2 << 20),
        name="final_sum",
    )(chip, *pieces, token)
    return grad_normed, weight_grads


def solution(mesh):
    n_dp, n_node = mesh.shape["dp"], mesh.shape["node"]

    def shards(*arrays):
        normed, gate_weight = arrays[0], arrays[2]
        rows, width = normed.shape
        hidden = gate_weight.shape[1]
        fits = (
            n_dp == 4
            and n_node == 8
            and rows * n_node == 16
            and hidden % 256 == 0
            and hidden * width * 6 <= 46 << 20
            and width % (n_dp * 256) == 0
        )
        if fits:
            return shards_group((n_dp, n_node), *arrays)
        return shards_any(n_dp, *arrays)

    in_specs = (
        P(("dp", "node"), None),
        P(("dp", "node"), None),
        P(None, "node"),
        P(None, "node"),
        P("node", None),
    )
    out_specs = (P(("dp", "node"), None), P("dp", "node"))
    return jax.shard_map(shards, mesh=mesh, in_specs=in_specs, out_specs=out_specs, check_vma=False)
```

```python
import jax
import jax.numpy as jnp
from jax import lax
from jax.experimental import pallas as pl
from jax.experimental.pallas import tpu as pltpu
from jax.sharding import PartitionSpec as P

BF = jnp.bfloat16
F32 = jnp.float32
NN = (((1,), (0,)), ((), ()))
NT = (((1,), (1,)), ((), ()))
TN = (((0,), (0,)), ((), ()))
ANY_SPEC = pl.BlockSpec(memory_space=pl.ANY)
HBM_SPEC = pl.BlockSpec(memory_space=pltpu.HBM)
VMEM_SPEC = pl.BlockSpec(memory_space=pltpu.VMEM)


def dot(left, right, dims):
    return lax.dot_general(left, right, dims, preferred_element_type=F32)


def in_hbm(array):
    return pltpu.with_memory_space_constraint(array, pltpu.HBM)


def in_vmem(array):
    return pltpu.with_memory_space_constraint(array, pltpu.VMEM)


def xor_pairs(count, step):
    return [(i, i ^ step) for i in range(count)]


def shards_any(n_dp, normed, cotangent, gate_weight, up_weight, down_weight):
    rows = lax.all_gather(normed, "node", axis=0, tiled=True)
    cots = lax.all_gather(cotangent, "node", axis=0, tiled=True)
    gate_pre = dot(rows, gate_weight, NN)
    up_pre = dot(rows, up_weight, NN)
    sigma = jax.nn.sigmoid(gate_pre)
    activated = gate_pre * sigma
    hidden = (activated * up_pre).astype(BF)
    grad_hidden = dot(cots, down_weight, NT)
    grad_gate = (grad_hidden * up_pre * sigma * (1.0 + gate_pre * (1.0 - sigma))).astype(BF)
    grad_up = (grad_hidden * activated).astype(BF)
    grad_normed = lax.psum_scatter(
        dot(grad_gate, gate_weight, NT) + dot(grad_up, up_weight, NT),
        "node",
        scatter_dimension=0,
        tiled=True,
    ).astype(BF)
    stacked = jnp.concatenate(
        [dot(rows, grad_gate, TN), dot(rows, grad_up, TN), dot(cots, hidden, TN)], axis=0
    )
    weight_grads = lax.psum_scatter(
        stacked.astype(BF), "dp", scatter_dimension=0, tiled=True
    ).astype(F32)
    return grad_normed, weight_grads


def load_kernel(first, count, weight, after, *refs):
    out, token, sem = refs[-3:]
    part = pl.ds(first, count)
    copy = pltpu.make_async_copy(weight.at[part], out.at[part], sem)
    copy.start()
    token[...] = jnp.zeros(token.shape, token.dtype)
    copy.wait()


def load_rows(weight, first, count, after, held, name):
    return pl.pallas_call(
        lambda *refs: load_kernel(first, count, *refs),
        out_shape=(
            pltpu.VMEM(weight.shape, weight.dtype),
            jax.ShapeDtypeStruct((8, 128), F32),
        ),
        in_specs=[HBM_SPEC, ANY_SPEC] + [VMEM_SPEC] * len(held),
        out_specs=(VMEM_SPEC, VMEM_SPEC),
        input_output_aliases={2: 0} if held else {},
        scratch_shapes=[pltpu.SemaphoreType.DMA],
        compiler_params=pltpu.CompilerParams(vmem_limit_bytes=1 << 20),
        cost_estimate=pl.CostEstimate(
            flops=0, bytes_accessed=2 * count * weight.shape[1], transcendentals=0
        ),
        name=name,
    )(weight, after, *held)


def pair_kernel(normed, cotangent, other_normed, other_cotangent, after, out):
    out[0, 0] = normed[...]
    out[0, 1] = cotangent[...]
    out[1, 0] = other_normed[...]
    out[1, 1] = other_cotangent[...]


def glue(kernel, shape, pieces, after, name):
    return pl.pallas_call(
        kernel,
        out_shape=jax.ShapeDtypeStruct(shape, BF),
        in_specs=[VMEM_SPEC] * len(pieces) + [ANY_SPEC],
        out_specs=VMEM_SPEC,
        compiler_params=pltpu.CompilerParams(vmem_limit_bytes=4 << 20),
        cost_estimate=pl.CostEstimate(flops=0, bytes_accessed=1 << 18, transcendentals=0),
        name=name,
    )(*pieces, after)


def arrange_kernel(n_dp, chips, *refs):
    sources, (tokens, *columns, wide) = refs[:chips], refs[chips + 1 :]
    own = sources[0].shape[2]
    unit = tokens.shape[2] // n_dp
    for i in range(2):
        for slot, source in enumerate(sources):
            for core in range(2):
                start = (core * chips + slot) * own
                wide[i, start : start + own] = source[core, i].astype(F32)
        tokens[i] = wide[i].astype(BF)
    for step, out in enumerate(columns):
        owner = lax.axis_index("dp") ^ step
        for j in range(3):
            index = 3 * owner + j
            part = pl.ds(pl.multiple_of(lax.rem(index, n_dp) * unit, unit), unit)
            out[:, j * unit : (j + 1) * unit] = tokens[lax.div(index, 2 * n_dp), :, part]


def forward_kernel(chunk, tokens, gate, down, up_hbm, grads, up, _, gate_pre, grad_hidden, sem):
    rows, columns = gate.shape
    parts = [slice(start, start + chunk) for start in range(0, columns, chunk)]
    piece = rows // sem.shape[0]
    copies = [
        pltpu.make_async_copy(
            up_hbm.at[pl.ds(i * piece, piece)], up.at[pl.ds(i * piece, piece)], sem.at[i]
        )
        for i in range(sem.shape[0])
    ]
    for copy in copies:
        copy.start(priority=1)
    for part in parts:
        gate_pre[:, part] = dot(tokens[0], gate[:, part], NN)
        grad_hidden[:, part] = dot(tokens[1], down[part, :], NT)
    for copy in copies:
        copy.wait()
    for part in parts:
        up_part = dot(tokens[0], up[:, part], NN)
        gate_part = gate_pre[:, part]
        sigma = jax.nn.sigmoid(gate_part)
        activated = gate_part * sigma
        grads[0, :, part] = (
            grad_hidden[:, part] * up_part * sigma * (1.0 + gate_part * (1.0 - sigma))
        ).astype(BF)
        grads[1, :, part] = (grad_hidden[:, part] * activated).astype(BF)
        grads[2, :, part] = (activated * up_part).astype(BF)


def pack_kernel(n_dp, grads, *refs):
    for step, pack in enumerate(refs[-n_dp:]):
        owner = lax.axis_index("dp") ^ step
        pack[0] = grads[lax.div(3 * owner, n_dp)]
        pack[1] = grads[lax.div(3 * owner + 2, n_dp)]


def backward_kernel(chunk, grads, gate, up, keep, send):
    rows = keep.shape[0]
    for start in range(0, gate.shape[0], chunk):
        part = slice(start, start + chunk)
        total = dot(grads[0], gate[part, :], NT) + dot(grads[1], up[part, :], NT)
        keep[:, part] = total[:rows]
        send[:, part] = total[rows:].astype(BF)


def product_kernel(n_dp, pieces, *refs):
    sources, packs = refs[:n_dp], refs[n_dp : 2 * n_dp]
    out, token, columns, grads, result, sem = refs[2 * n_dp :]
    group, block = sources[0].shape
    unit = block // 3
    d = lax.axis_index("dp")
    token[...] = jnp.zeros(token.shape, token.dtype)
    for slot in range(n_dp):
        rows = slice(slot * group, (slot + 1) * group)
        columns[rows] = sources[slot][...]
        for m in range(2):
            grads[m, rows] = packs[slot][m]
    copies = []
    for i, (start, count) in enumerate(pieces):
        j = start // unit
        which = lax.div(3 * d + j, n_dp) - lax.div(3 * d, n_dp)
        part = slice(start, start + count)
        result[part] = dot(columns[:, part], grads[which], TN)
        copy = pltpu.make_async_copy(
            result.at[pl.ds(start, count)], out.at[pl.ds(start, count)], sem.at[i]
        )
        copy.start()
        copies.append(copy)
    for copy in copies:
        copy.wait()


def hold_kernel(piece, *refs):
    refs[-1][...] = piece[...]


def final_kernel(own, chip, first, second, third, after, out):
    total = chip[:own]
    for piece in (first, second, third):
        total = total + piece[...].astype(F32)
    out[...] = total.astype(BF)


def shards_group(mesh_shape, normed, cotangent, gate_weight, up_weight, down_weight):
    n_dp, n_node = mesh_shape
    own, width = normed.shape
    hidden = gate_weight.shape[1]
    group = own * n_node
    block = 3 * width // n_dp
    half, quarter = width // 2, width // 4
    chips = range(2, n_node, 2)
    groups = range(1, n_dp)
    weight_bytes = 2 * width * hidden

    def permute(array, axis, step):
        return lax.ppermute(array, axis, xor_pairs(mesh_shape[axis == "node"], step))

    gate_hbm, up_hbm = in_hbm(gate_weight), in_hbm(up_weight)
    others = [permute(array, "node", 1) for array in (normed, cotangent)]
    gate, token = load_rows(gate_hbm, 0, quarter, in_hbm(normed), (), "load_gate_a")
    pair = glue(
        pair_kernel, (2, 2, own, width), [normed, cotangent, *others], token, "pair"
    )
    plane = [pair] + [permute(pair, "node", s) for s in chips]
    gate, token = load_rows(
        gate_hbm, quarter, width - quarter, token, (in_vmem(gate),), "load_gate_b"
    )
    piece = jax.ShapeDtypeStruct((group, block), BF)
    tokens, *columns = pl.pallas_call(
        lambda *refs: arrange_kernel(n_dp, len(plane), *refs),
        out_shape=[jax.ShapeDtypeStruct((2, group, width), BF)] + [piece] * n_dp,
        in_specs=[VMEM_SPEC] * len(plane) + [ANY_SPEC],
        out_specs=[VMEM_SPEC] * (n_dp + 1),
        scratch_shapes=[pltpu.VMEM((2, group, width), F32)],
        compiler_params=pltpu.CompilerParams(vmem_limit_bytes=4 << 20),
        cost_estimate=pl.CostEstimate(flops=0, bytes_accessed=1 << 20, transcendentals=0),
        name="arrange",
    )(*plane, token)
    columns = [columns[0]] + [permute(columns[s], "dp", s) for s in groups]

    chunk = 256
    grads, up, gate = pl.pallas_call(
        lambda *refs: forward_kernel(chunk, *refs),
        out_shape=[
            jax.ShapeDtypeStruct((3, group, hidden), BF),
            pltpu.VMEM((width, hidden), BF),
            pltpu.VMEM((width, hidden), BF),
        ],
        in_specs=[VMEM_SPEC] * 3 + [HBM_SPEC],
        out_specs=[VMEM_SPEC] * 3,
        input_output_aliases={1: 2},
        scratch_shapes=[
            pltpu.VMEM((group, hidden), F32),
            pltpu.VMEM((group, hidden), F32),
            pltpu.SemaphoreType.DMA((8,)),
        ],
        compiler_params=pltpu.CompilerParams(vmem_limit_bytes=4 << 20),
        cost_estimate=pl.CostEstimate(
            flops=6 * group * width * hidden, bytes_accessed=2 * weight_bytes, transcendentals=0
        ),
        name="forward",
    )(tokens, in_vmem(gate), in_vmem(down_weight), up_hbm)

    packs = pl.pallas_call(
        lambda *refs: pack_kernel(n_dp, *refs),
        out_shape=[jax.ShapeDtypeStruct((2, group, hidden), BF)] * n_dp,
        in_specs=[VMEM_SPEC] + [ANY_SPEC] * (n_dp - 1),
        out_specs=[VMEM_SPEC] * n_dp,
        compiler_params=pltpu.CompilerParams(vmem_limit_bytes=1 << 20),
        name="pack",
    )(grads, *columns[1:])
    packs = [packs[0]] + [permute(packs[s], "dp", s) for s in groups]

    keep, send = pl.pallas_call(
        lambda *refs: backward_kernel(chunk, *refs),
        out_shape=(
            jax.ShapeDtypeStruct((group // 2, width), F32),
            jax.ShapeDtypeStruct((group // 2, width), BF),
        ),
        in_specs=[VMEM_SPEC] * 3,
        out_specs=(VMEM_SPEC, VMEM_SPEC),
        compiler_params=pltpu.CompilerParams(vmem_limit_bytes=4 << 20),
        cost_estimate=pl.CostEstimate(
            flops=4 * group * width * hidden, bytes_accessed=2 * weight_bytes, transcendentals=0
        ),
        name="backward",
    )(grads, in_vmem(gate), in_vmem(up))

    send = pl.pallas_call(
        hold_kernel,
        out_shape=jax.ShapeDtypeStruct(send.shape, BF),
        in_specs=[VMEM_SPEC] + [ANY_SPEC] * (n_dp - 1),
        out_specs=VMEM_SPEC,
        compiler_params=pltpu.CompilerParams(vmem_limit_bytes=1 << 20),
        name="hold",
    )(send, *packs[1:])
    chip = keep + permute(send, "node", 1).astype(F32)
    pieces = [
        permute(chip[own * slot : own * (slot + 1)].astype(BF), "node", s)
        for slot, s in enumerate(chips, 1)
    ]

    cuts = [(start, 256) for start in range(0, block, 256)]
    weight_grads, token = pl.pallas_call(
        lambda *refs: product_kernel(n_dp, cuts, *refs),
        out_shape=(
            pltpu.HBM((block, hidden), F32),
            jax.ShapeDtypeStruct((8, 128), F32),
        ),
        in_specs=[VMEM_SPEC] * (2 * n_dp),
        out_specs=(HBM_SPEC, VMEM_SPEC),
        scratch_shapes=[
            pltpu.VMEM((n_dp * group, block), BF),
            pltpu.VMEM((2, n_dp * group, hidden), BF),
            pltpu.VMEM((block, hidden), F32),
            pltpu.SemaphoreType.DMA((len(cuts),)),
        ],
        compiler_params=pltpu.CompilerParams(vmem_limit_bytes=32 << 20),
        cost_estimate=pl.CostEstimate(
            flops=2 * n_dp * group * block * hidden,
            bytes_accessed=4 * block * hidden,
            transcendentals=0,
        ),
        name="product",
    )(*columns, *packs)
    grad_normed = pl.pallas_call(
        lambda *refs: final_kernel(own, *refs),
        out_shape=jax.ShapeDtypeStruct((own, width), BF),
        in_specs=[VMEM_SPEC] * 4 + [ANY_SPEC],
        out_specs=VMEM_SPEC,
        compiler_params=pltpu.CompilerParams(vmem_limit_bytes=2 << 20),
        name="final_sum",
    )(chip, *pieces, token)
    return grad_normed, weight_grads


def solution(mesh):
    n_dp, n_node = mesh.shape["dp"], mesh.shape["node"]

    def shards(*arrays):
        normed, gate_weight = arrays[0], arrays[2]
        rows, width = normed.shape
        hidden = gate_weight.shape[1]
        fits = (
            n_dp == 4
            and n_node == 8
            and rows * n_node == 16
            and hidden % 256 == 0
            and hidden * width * 6 <= 46 << 20
            and width % (n_dp * 256) == 0
        )
        if fits:
            return shards_group((n_dp, n_node), *arrays)
        return shards_any(n_dp, *arrays)

    in_specs = (
        P(("dp", "node"), None),
        P(("dp", "node"), None),
        P(None, "node"),
        P(None, "node"),
        P("node", None),
    )
    out_specs = (P(("dp", "node"), None), P("dp", "node"))
    return jax.shard_map(shards, mesh=mesh, in_specs=in_specs, out_specs=out_specs, check_vma=False)
```

```python
import jax
import jax.numpy as jnp
from jax import lax
from jax.experimental import pallas as pl
from jax.experimental.pallas import tpu as pltpu
from jax.sharding import PartitionSpec as P

BF = jnp.bfloat16
F32 = jnp.float32
NN = (((1,), (0,)), ((), ()))
NT = (((1,), (1,)), ((), ()))
TN = (((0,), (0,)), ((), ()))
ANY_SPEC = pl.BlockSpec(memory_space=pl.ANY)
HBM_SPEC = pl.BlockSpec(memory_space=pltpu.HBM)
VMEM_SPEC = pl.BlockSpec(memory_space=pltpu.VMEM)


def dot(left, right, dims):
    return lax.dot_general(left, right, dims, preferred_element_type=F32)


def in_hbm(array):
    return pltpu.with_memory_space_constraint(array, pltpu.HBM)


def in_vmem(array):
    return pltpu.with_memory_space_constraint(array, pltpu.VMEM)


def xor_pairs(count, step):
    return [(i, i ^ step) for i in range(count)]


def shards_any(n_dp, normed, cotangent, gate_weight, up_weight, down_weight):
    rows = lax.all_gather(normed, "node", axis=0, tiled=True)
    cots = lax.all_gather(cotangent, "node", axis=0, tiled=True)
    gate_pre = dot(rows, gate_weight, NN)
    up_pre = dot(rows, up_weight, NN)
    sigma = jax.nn.sigmoid(gate_pre)
    activated = gate_pre * sigma
    hidden = (activated * up_pre).astype(BF)
    grad_hidden = dot(cots, down_weight, NT)
    grad_gate = (grad_hidden * up_pre * sigma * (1.0 + gate_pre * (1.0 - sigma))).astype(BF)
    grad_up = (grad_hidden * activated).astype(BF)
    grad_normed = lax.psum_scatter(
        dot(grad_gate, gate_weight, NT) + dot(grad_up, up_weight, NT),
        "node",
        scatter_dimension=0,
        tiled=True,
    ).astype(BF)
    stacked = jnp.concatenate(
        [dot(rows, grad_gate, TN), dot(rows, grad_up, TN), dot(cots, hidden, TN)], axis=0
    )
    weight_grads = lax.psum_scatter(
        stacked.astype(BF), "dp", scatter_dimension=0, tiled=True
    ).astype(F32)
    return grad_normed, weight_grads


def load_kernel(first, count, weight, after, *refs):
    out, token, sem = refs[-3:]
    part = pl.ds(first, count)
    copy = pltpu.make_async_copy(weight.at[part], out.at[part], sem)
    copy.start()
    token[...] = jnp.zeros(token.shape, token.dtype)
    copy.wait()


def load_rows(weight, first, count, after, held, name):
    return pl.pallas_call(
        lambda *refs: load_kernel(first, count, *refs),
        out_shape=(
            pltpu.VMEM(weight.shape, weight.dtype),
            jax.ShapeDtypeStruct((8, 128), F32),
        ),
        in_specs=[HBM_SPEC, ANY_SPEC] + [VMEM_SPEC] * len(held),
        out_specs=(VMEM_SPEC, VMEM_SPEC),
        input_output_aliases={2: 0} if held else {},
        scratch_shapes=[pltpu.SemaphoreType.DMA],
        compiler_params=pltpu.CompilerParams(vmem_limit_bytes=1 << 20),
        cost_estimate=pl.CostEstimate(
            flops=0, bytes_accessed=2 * count * weight.shape[1], transcendentals=0
        ),
        name=name,
    )(weight, after, *held)


def pair_kernel(normed, cotangent, other_normed, other_cotangent, after, out):
    out[0, 0] = normed[...]
    out[0, 1] = cotangent[...]
    out[1, 0] = other_normed[...]
    out[1, 1] = other_cotangent[...]


def glue(kernel, shape, pieces, after, name):
    return pl.pallas_call(
        kernel,
        out_shape=jax.ShapeDtypeStruct(shape, BF),
        in_specs=[VMEM_SPEC] * len(pieces) + [ANY_SPEC],
        out_specs=VMEM_SPEC,
        compiler_params=pltpu.CompilerParams(vmem_limit_bytes=4 << 20),
        cost_estimate=pl.CostEstimate(flops=0, bytes_accessed=1 << 18, transcendentals=0),
        name=name,
    )(*pieces, after)


def arrange_kernel(n_dp, chips, *refs):
    sources, (tokens, *columns, wide) = refs[:chips], refs[chips + 1 :]
    own = sources[0].shape[2]
    unit = tokens.shape[2] // n_dp
    for i in range(2):
        for slot, source in enumerate(sources):
            for core in range(2):
                start = (core * chips + slot) * own
                wide[i, start : start + own] = source[core, i].astype(F32)
        tokens[i] = wide[i].astype(BF)
    for step, out in enumerate(columns):
        owner = lax.axis_index("dp") ^ step
        for j in range(3):
            index = 3 * owner + j
            part = pl.ds(pl.multiple_of(lax.rem(index, n_dp) * unit, unit), unit)
            out[:, j * unit : (j + 1) * unit] = tokens[lax.div(index, 2 * n_dp), :, part]


def forward_kernel(chunk, tokens, gate, down, up_hbm, grads, up, _, gate_pre, grad_hidden, sem):
    rows, columns = gate.shape
    parts = [slice(start, start + chunk) for start in range(0, columns, chunk)]
    piece = rows // sem.shape[0]
    copies = [
        pltpu.make_async_copy(
            up_hbm.at[pl.ds(i * piece, piece)], up.at[pl.ds(i * piece, piece)], sem.at[i]
        )
        for i in range(sem.shape[0])
    ]
    for copy in copies:
        copy.start(priority=1)
    for part in parts:
        gate_pre[:, part] = dot(tokens[0], gate[:, part], NN)
        grad_hidden[:, part] = dot(tokens[1], down[part, :], NT)
    for copy in copies:
        copy.wait()
    for part in parts:
        up_part = dot(tokens[0], up[:, part], NN)
        gate_part = gate_pre[:, part]
        sigma = jax.nn.sigmoid(gate_part)
        activated = gate_part * sigma
        grads[0, :, part] = (
            grad_hidden[:, part] * up_part * sigma * (1.0 + gate_part * (1.0 - sigma))
        ).astype(BF)
        grads[1, :, part] = (grad_hidden[:, part] * activated).astype(BF)
        grads[2, :, part] = (activated * up_part).astype(BF)


def pack_kernel(n_dp, grads, *refs):
    for step, pack in enumerate(refs[-n_dp:]):
        owner = lax.axis_index("dp") ^ step
        pack[0] = grads[lax.div(3 * owner, n_dp)]
        pack[1] = grads[lax.div(3 * owner + 2, n_dp)]


def backward_kernel(chunk, grads, gate, up, keep, send):
    rows = keep.shape[0]
    for start in range(0, gate.shape[0], chunk):
        part = slice(start, start + chunk)
        total = dot(grads[0], gate[part, :], NT) + dot(grads[1], up[part, :], NT)
        keep[:, part] = total[:rows]
        send[:, part] = total[rows:].astype(BF)


def product_kernel(n_dp, pieces, *refs):
    sources, packs = refs[:n_dp], refs[n_dp : 2 * n_dp]
    out, token, columns, grads, result, sem = refs[2 * n_dp :]
    group, block = sources[0].shape
    unit = block // 3
    d = lax.axis_index("dp")
    token[...] = jnp.zeros(token.shape, token.dtype)
    for slot in range(n_dp):
        rows = slice(slot * group, (slot + 1) * group)
        columns[rows] = sources[slot][...]
        for m in range(2):
            grads[m, rows] = packs[slot][m]
    copies = []
    for i, (start, count) in enumerate(pieces):
        j = start // unit
        which = lax.div(3 * d + j, n_dp) - lax.div(3 * d, n_dp)
        part = slice(start, start + count)
        result[part] = dot(columns[:, part], grads[which], TN)
        copy = pltpu.make_async_copy(
            result.at[pl.ds(start, count)], out.at[pl.ds(start, count)], sem.at[i]
        )
        copy.start(priority=i % 2)
        copies.append(copy)
    for copy in copies:
        copy.wait()


def hold_kernel(piece, *refs):
    refs[-1][...] = piece[...]


def final_kernel(own, chip, first, second, third, after, out):
    total = chip[:own]
    for piece in (first, second, third):
        total = total + piece[...].astype(F32)
    out[...] = total.astype(BF)


def shards_group(mesh_shape, normed, cotangent, gate_weight, up_weight, down_weight):
    n_dp, n_node = mesh_shape
    own, width = normed.shape
    hidden = gate_weight.shape[1]
    group = own * n_node
    block = 3 * width // n_dp
    half, quarter = width // 2, width // 4
    chips = range(2, n_node, 2)
    groups = range(1, n_dp)
    weight_bytes = 2 * width * hidden

    def permute(array, axis, step):
        return lax.ppermute(array, axis, xor_pairs(mesh_shape[axis == "node"], step))

    gate_hbm, up_hbm = in_hbm(gate_weight), in_hbm(up_weight)
    others = [permute(array, "node", 1) for array in (normed, cotangent)]
    gate, token = load_rows(gate_hbm, 0, quarter, in_hbm(normed), (), "load_gate_a")
    pair = glue(
        pair_kernel, (2, 2, own, width), [normed, cotangent, *others], token, "pair"
    )
    plane = [pair] + [permute(pair, "node", s) for s in chips]
    gate, token = load_rows(
        gate_hbm, quarter, width - quarter, token, (in_vmem(gate),), "load_gate_b"
    )
    piece = jax.ShapeDtypeStruct((group, block), BF)
    tokens, *columns = pl.pallas_call(
        lambda *refs: arrange_kernel(n_dp, len(plane), *refs),
        out_shape=[jax.ShapeDtypeStruct((2, group, width), BF)] + [piece] * n_dp,
        in_specs=[VMEM_SPEC] * len(plane) + [ANY_SPEC],
        out_specs=[VMEM_SPEC] * (n_dp + 1),
        scratch_shapes=[pltpu.VMEM((2, group, width), F32)],
        compiler_params=pltpu.CompilerParams(vmem_limit_bytes=4 << 20),
        cost_estimate=pl.CostEstimate(flops=0, bytes_accessed=1 << 20, transcendentals=0),
        name="arrange",
    )(*plane, token)
    columns = [columns[0]] + [permute(columns[s], "dp", s) for s in groups]

    chunk = 256
    grads, up, gate = pl.pallas_call(
        lambda *refs: forward_kernel(chunk, *refs),
        out_shape=[
            jax.ShapeDtypeStruct((3, group, hidden), BF),
            pltpu.VMEM((width, hidden), BF),
            pltpu.VMEM((width, hidden), BF),
        ],
        in_specs=[VMEM_SPEC] * 3 + [HBM_SPEC],
        out_specs=[VMEM_SPEC] * 3,
        input_output_aliases={1: 2},
        scratch_shapes=[
            pltpu.VMEM((group, hidden), F32),
            pltpu.VMEM((group, hidden), F32),
            pltpu.SemaphoreType.DMA((8,)),
        ],
        compiler_params=pltpu.CompilerParams(vmem_limit_bytes=4 << 20),
        cost_estimate=pl.CostEstimate(
            flops=6 * group * width * hidden, bytes_accessed=2 * weight_bytes, transcendentals=0
        ),
        name="forward",
    )(tokens, in_vmem(gate), in_vmem(down_weight), up_hbm)

    packs = pl.pallas_call(
        lambda *refs: pack_kernel(n_dp, *refs),
        out_shape=[jax.ShapeDtypeStruct((2, group, hidden), BF)] * n_dp,
        in_specs=[VMEM_SPEC] + [ANY_SPEC] * (n_dp - 1),
        out_specs=[VMEM_SPEC] * n_dp,
        compiler_params=pltpu.CompilerParams(vmem_limit_bytes=1 << 20),
        name="pack",
    )(grads, *columns[1:])
    packs = [packs[0]] + [permute(packs[s], "dp", s) for s in groups]

    keep, send = pl.pallas_call(
        lambda *refs: backward_kernel(chunk, *refs),
        out_shape=(
            jax.ShapeDtypeStruct((group // 2, width), F32),
            jax.ShapeDtypeStruct((group // 2, width), BF),
        ),
        in_specs=[VMEM_SPEC] * 3,
        out_specs=(VMEM_SPEC, VMEM_SPEC),
        compiler_params=pltpu.CompilerParams(vmem_limit_bytes=4 << 20),
        cost_estimate=pl.CostEstimate(
            flops=4 * group * width * hidden, bytes_accessed=2 * weight_bytes, transcendentals=0
        ),
        name="backward",
    )(grads, in_vmem(gate), in_vmem(up))

    send = pl.pallas_call(
        hold_kernel,
        out_shape=jax.ShapeDtypeStruct(send.shape, BF),
        in_specs=[VMEM_SPEC] + [ANY_SPEC] * (n_dp - 1),
        out_specs=VMEM_SPEC,
        compiler_params=pltpu.CompilerParams(vmem_limit_bytes=1 << 20),
        name="hold",
    )(send, *packs[1:])
    chip = keep + permute(send, "node", 1).astype(F32)
    pieces = [
        permute(chip[own * slot : own * (slot + 1)].astype(BF), "node", s)
        for slot, s in enumerate(chips, 1)
    ]

    cuts = [(0, 128), (128, 128)] + [(start, 256) for start in range(256, block, 256)]
    weight_grads, token = pl.pallas_call(
        lambda *refs: product_kernel(n_dp, cuts, *refs),
        out_shape=(
            pltpu.HBM((block, hidden), F32),
            jax.ShapeDtypeStruct((8, 128), F32),
        ),
        in_specs=[VMEM_SPEC] * (2 * n_dp),
        out_specs=(HBM_SPEC, VMEM_SPEC),
        scratch_shapes=[
            pltpu.VMEM((n_dp * group, block), BF),
            pltpu.VMEM((2, n_dp * group, hidden), BF),
            pltpu.VMEM((block, hidden), F32),
            pltpu.SemaphoreType.DMA((len(cuts),)),
        ],
        compiler_params=pltpu.CompilerParams(vmem_limit_bytes=32 << 20),
        cost_estimate=pl.CostEstimate(
            flops=2 * n_dp * group * block * hidden,
            bytes_accessed=4 * block * hidden,
            transcendentals=0,
        ),
        name="product",
    )(*columns, *packs)
    grad_normed = pl.pallas_call(
        lambda *refs: final_kernel(own, *refs),
        out_shape=jax.ShapeDtypeStruct((own, width), BF),
        in_specs=[VMEM_SPEC] * 4 + [ANY_SPEC],
        out_specs=VMEM_SPEC,
        compiler_params=pltpu.CompilerParams(vmem_limit_bytes=2 << 20),
        name="final_sum",
    )(chip, *pieces, token)
    return grad_normed, weight_grads


def solution(mesh):
    n_dp, n_node = mesh.shape["dp"], mesh.shape["node"]

    def shards(*arrays):
        normed, gate_weight = arrays[0], arrays[2]
        rows, width = normed.shape
        hidden = gate_weight.shape[1]
        fits = (
            n_dp == 4
            and n_node == 8
            and rows * n_node == 16
            and hidden % 256 == 0
            and hidden * width * 6 <= 46 << 20
            and width % (n_dp * 256) == 0
        )
        if fits:
            return shards_group((n_dp, n_node), *arrays)
        return shards_any(n_dp, *arrays)

    in_specs = (
        P(("dp", "node"), None),
        P(("dp", "node"), None),
        P(None, "node"),
        P(None, "node"),
        P("node", None),
    )
    out_specs = (P(("dp", "node"), None), P("dp", "node"))
    return jax.shard_map(shards, mesh=mesh, in_specs=in_specs, out_specs=out_specs, check_vma=False)
```

```python
import jax
import jax.numpy as jnp
from jax import lax
from jax.experimental import pallas as pl
from jax.experimental.pallas import tpu as pltpu
from jax.sharding import PartitionSpec as P

BF = jnp.bfloat16
F32 = jnp.float32
NN = (((1,), (0,)), ((), ()))
NT = (((1,), (1,)), ((), ()))
TN = (((0,), (0,)), ((), ()))
ANY_SPEC = pl.BlockSpec(memory_space=pl.ANY)
HBM_SPEC = pl.BlockSpec(memory_space=pltpu.HBM)
VMEM_SPEC = pl.BlockSpec(memory_space=pltpu.VMEM)


def dot(left, right, dims):
    return lax.dot_general(left, right, dims, preferred_element_type=F32)


def in_hbm(array):
    return pltpu.with_memory_space_constraint(array, pltpu.HBM)


def in_vmem(array):
    return pltpu.with_memory_space_constraint(array, pltpu.VMEM)


def xor_pairs(count, step):
    return [(i, i ^ step) for i in range(count)]


def shards_any(n_dp, normed, cotangent, gate_weight, up_weight, down_weight):
    rows = lax.all_gather(normed, "node", axis=0, tiled=True)
    cots = lax.all_gather(cotangent, "node", axis=0, tiled=True)
    gate_pre = dot(rows, gate_weight, NN)
    up_pre = dot(rows, up_weight, NN)
    sigma = jax.nn.sigmoid(gate_pre)
    activated = gate_pre * sigma
    hidden = (activated * up_pre).astype(BF)
    grad_hidden = dot(cots, down_weight, NT)
    grad_gate = (grad_hidden * up_pre * sigma * (1.0 + gate_pre * (1.0 - sigma))).astype(BF)
    grad_up = (grad_hidden * activated).astype(BF)
    grad_normed = lax.psum_scatter(
        dot(grad_gate, gate_weight, NT) + dot(grad_up, up_weight, NT),
        "node",
        scatter_dimension=0,
        tiled=True,
    ).astype(BF)
    stacked = jnp.concatenate(
        [dot(rows, grad_gate, TN), dot(rows, grad_up, TN), dot(cots, hidden, TN)], axis=0
    )
    weight_grads = lax.psum_scatter(
        stacked.astype(BF), "dp", scatter_dimension=0, tiled=True
    ).astype(F32)
    return grad_normed, weight_grads


def load_kernel(first, count, weight, after, *refs):
    out, token, sem = refs[-3:]
    piece = count // sem.shape[0]
    copies = []
    for i in range(sem.shape[0]):
        part = pl.ds(first + i * piece, piece)
        copies.append(pltpu.make_async_copy(weight.at[part], out.at[part], sem.at[i]))
    for copy in copies:
        copy.start(priority=1)
    token[...] = jnp.zeros(token.shape, token.dtype)
    for copy in copies:
        copy.wait()


def load_rows(weight, first, count, after, held, name):
    return pl.pallas_call(
        lambda *refs: load_kernel(first, count, *refs),
        out_shape=(
            pltpu.VMEM(weight.shape, weight.dtype),
            jax.ShapeDtypeStruct((8, 128), F32),
        ),
        in_specs=[HBM_SPEC, ANY_SPEC] + [VMEM_SPEC] * len(held),
        out_specs=(VMEM_SPEC, VMEM_SPEC),
        input_output_aliases={2: 0} if held else {},
        scratch_shapes=[pltpu.SemaphoreType.DMA((8,))],
        compiler_params=pltpu.CompilerParams(vmem_limit_bytes=1 << 20),
        cost_estimate=pl.CostEstimate(
            flops=0, bytes_accessed=2 * count * weight.shape[1], transcendentals=0
        ),
        name=name,
    )(weight, after, *held)


def pair_kernel(normed, cotangent, other_normed, other_cotangent, after, out):
    out[0, 0] = normed[...]
    out[0, 1] = cotangent[...]
    out[1, 0] = other_normed[...]
    out[1, 1] = other_cotangent[...]


def glue(kernel, shape, pieces, after, name):
    return pl.pallas_call(
        kernel,
        out_shape=jax.ShapeDtypeStruct(shape, BF),
        in_specs=[VMEM_SPEC] * len(pieces) + [ANY_SPEC],
        out_specs=VMEM_SPEC,
        compiler_params=pltpu.CompilerParams(vmem_limit_bytes=4 << 20),
        cost_estimate=pl.CostEstimate(flops=0, bytes_accessed=1 << 18, transcendentals=0),
        name=name,
    )(*pieces, after)


def arrange_kernel(n_dp, chips, *refs):
    sources, (tokens, *columns, wide) = refs[:chips], refs[chips + 1 :]
    own = sources[0].shape[2]
    unit = tokens.shape[2] // n_dp
    for i in range(2):
        for slot, source in enumerate(sources):
            for core in range(2):
                start = (core * chips + slot) * own
                wide[i, start : start + own] = source[core, i].astype(F32)
        tokens[i] = wide[i].astype(BF)
    for step, out in enumerate(columns):
        owner = lax.axis_index("dp") ^ step
        for j in range(3):
            index = 3 * owner + j
            part = pl.ds(pl.multiple_of(lax.rem(index, n_dp) * unit, unit), unit)
            out[:, j * unit : (j + 1) * unit] = tokens[lax.div(index, 2 * n_dp), :, part]


def forward_kernel(chunk, tokens, gate, down, up_hbm, grads, up, _, gate_pre, grad_hidden, sem):
    rows, columns = gate.shape
    parts = [slice(start, start + chunk) for start in range(0, columns, chunk)]
    piece = rows // sem.shape[0]
    copies = [
        pltpu.make_async_copy(
            up_hbm.at[pl.ds(i * piece, piece)], up.at[pl.ds(i * piece, piece)], sem.at[i]
        )
        for i in range(sem.shape[0])
    ]
    for copy in copies:
        copy.start(priority=1)
    for part in parts:
        gate_pre[:, part] = dot(tokens[0], gate[:, part], NN)
        grad_hidden[:, part] = dot(tokens[1], down[part, :], NT)
    for copy in copies:
        copy.wait()
    for part in parts:
        up_part = dot(tokens[0], up[:, part], NN)
        gate_part = gate_pre[:, part]
        sigma = jax.nn.sigmoid(gate_part)
        activated = gate_part * sigma
        grads[0, :, part] = (
            grad_hidden[:, part] * up_part * sigma * (1.0 + gate_part * (1.0 - sigma))
        ).astype(BF)
        grads[1, :, part] = (grad_hidden[:, part] * activated).astype(BF)
        grads[2, :, part] = (activated * up_part).astype(BF)


def pack_kernel(n_dp, grads, *refs):
    for step, pack in enumerate(refs[-n_dp:]):
        owner = lax.axis_index("dp") ^ step
        pack[0] = grads[lax.div(3 * owner, n_dp)]
        pack[1] = grads[lax.div(3 * owner + 2, n_dp)]


def backward_kernel(chunk, grads, gate, up, keep, send):
    rows = keep.shape[0]
    for start in range(0, gate.shape[0], chunk):
        part = slice(start, start + chunk)
        total = dot(grads[0], gate[part, :], NT) + dot(grads[1], up[part, :], NT)
        keep[:, part] = total[:rows]
        send[:, part] = total[rows:].astype(BF)


def product_kernel(n_dp, pieces, *refs):
    sources, packs = refs[:n_dp], refs[n_dp : 2 * n_dp]
    out, token, columns, grads, result, sem = refs[2 * n_dp :]
    group, block = sources[0].shape
    unit = block // 3
    d = lax.axis_index("dp")
    token[...] = jnp.zeros(token.shape, token.dtype)
    for slot in range(n_dp):
        rows = slice(slot * group, (slot + 1) * group)
        columns[rows] = sources[slot][...]
        for m in range(2):
            grads[m, rows] = packs[slot][m]
    copies = []
    for i, (start, count) in enumerate(pieces):
        j = start // unit
        which = lax.div(3 * d + j, n_dp) - lax.div(3 * d, n_dp)
        part = slice(start, start + count)
        result[part] = dot(columns[:, part], grads[which], TN)
        copy = pltpu.make_async_copy(
            result.at[pl.ds(start, count)], out.at[pl.ds(start, count)], sem.at[i]
        )
        copy.start()
        copies.append(copy)
    for copy in copies:
        copy.wait()


def hold_kernel(piece, *refs):
    refs[-1][...] = piece[...]


def final_kernel(own, chip, first, second, third, after, out):
    total = chip[:own]
    for piece in (first, second, third):
        total = total + piece[...].astype(F32)
    out[...] = total.astype(BF)


def shards_group(mesh_shape, normed, cotangent, gate_weight, up_weight, down_weight):
    n_dp, n_node = mesh_shape
    own, width = normed.shape
    hidden = gate_weight.shape[1]
    group = own * n_node
    block = 3 * width // n_dp
    half, quarter = width // 2, width // 8
    chips = range(2, n_node, 2)
    groups = range(1, n_dp)
    weight_bytes = 2 * width * hidden

    def permute(array, axis, step):
        return lax.ppermute(array, axis, xor_pairs(mesh_shape[axis == "node"], step))

    gate_hbm, up_hbm = in_hbm(gate_weight), in_hbm(up_weight)
    others = [permute(array, "node", 1) for array in (normed, cotangent)]
    gate, token = load_rows(gate_hbm, 0, quarter, in_hbm(normed), (), "load_gate_a")
    pair = glue(
        pair_kernel, (2, 2, own, width), [normed, cotangent, *others], token, "pair"
    )
    plane = [pair] + [permute(pair, "node", s) for s in chips]
    gate, token = load_rows(
        gate_hbm, quarter, width - quarter, token, (in_vmem(gate),), "load_gate_b"
    )
    piece = jax.ShapeDtypeStruct((group, block), BF)
    tokens, *columns = pl.pallas_call(
        lambda *refs: arrange_kernel(n_dp, len(plane), *refs),
        out_shape=[jax.ShapeDtypeStruct((2, group, width), BF)] + [piece] * n_dp,
        in_specs=[VMEM_SPEC] * len(plane) + [ANY_SPEC],
        out_specs=[VMEM_SPEC] * (n_dp + 1),
        scratch_shapes=[pltpu.VMEM((2, group, width), F32)],
        compiler_params=pltpu.CompilerParams(vmem_limit_bytes=4 << 20),
        cost_estimate=pl.CostEstimate(flops=0, bytes_accessed=1 << 20, transcendentals=0),
        name="arrange",
    )(*plane, token)
    columns = [columns[0]] + [permute(columns[s], "dp", s) for s in groups]

    chunk = 256
    grads, up, gate = pl.pallas_call(
        lambda *refs: forward_kernel(chunk, *refs),
        out_shape=[
            jax.ShapeDtypeStruct((3, group, hidden), BF),
            pltpu.VMEM((width, hidden), BF),
            pltpu.VMEM((width, hidden), BF),
        ],
        in_specs=[VMEM_SPEC] * 3 + [HBM_SPEC],
        out_specs=[VMEM_SPEC] * 3,
        input_output_aliases={1: 2},
        scratch_shapes=[
            pltpu.VMEM((group, hidden), F32),
            pltpu.VMEM((group, hidden), F32),
            pltpu.SemaphoreType.DMA((8,)),
        ],
        compiler_params=pltpu.CompilerParams(vmem_limit_bytes=4 << 20),
        cost_estimate=pl.CostEstimate(
            flops=6 * group * width * hidden, bytes_accessed=2 * weight_bytes, transcendentals=0
        ),
        name="forward",
    )(tokens, in_vmem(gate), in_vmem(down_weight), up_hbm)

    packs = pl.pallas_call(
        lambda *refs: pack_kernel(n_dp, *refs),
        out_shape=[jax.ShapeDtypeStruct((2, group, hidden), BF)] * n_dp,
        in_specs=[VMEM_SPEC] + [ANY_SPEC] * (n_dp - 1),
        out_specs=[VMEM_SPEC] * n_dp,
        compiler_params=pltpu.CompilerParams(vmem_limit_bytes=1 << 20),
        name="pack",
    )(grads, *columns[1:])
    packs = [packs[0]] + [permute(packs[s], "dp", s) for s in groups]

    keep, send = pl.pallas_call(
        lambda *refs: backward_kernel(chunk, *refs),
        out_shape=(
            jax.ShapeDtypeStruct((group // 2, width), F32),
            jax.ShapeDtypeStruct((group // 2, width), BF),
        ),
        in_specs=[VMEM_SPEC] * 3,
        out_specs=(VMEM_SPEC, VMEM_SPEC),
        compiler_params=pltpu.CompilerParams(vmem_limit_bytes=4 << 20),
        cost_estimate=pl.CostEstimate(
            flops=4 * group * width * hidden, bytes_accessed=2 * weight_bytes, transcendentals=0
        ),
        name="backward",
    )(grads, in_vmem(gate), in_vmem(up))

    send = pl.pallas_call(
        hold_kernel,
        out_shape=jax.ShapeDtypeStruct(send.shape, BF),
        in_specs=[VMEM_SPEC] + [ANY_SPEC] * (n_dp - 1),
        out_specs=VMEM_SPEC,
        compiler_params=pltpu.CompilerParams(vmem_limit_bytes=1 << 20),
        name="hold",
    )(send, *packs[1:])
    chip = keep + permute(send, "node", 1).astype(F32)
    pieces = [
        permute(chip[own * slot : own * (slot + 1)].astype(BF), "node", s)
        for slot, s in enumerate(chips, 1)
    ]

    cuts = [(start, 256) for start in range(0, block, 256)]
    weight_grads, token = pl.pallas_call(
        lambda *refs: product_kernel(n_dp, cuts, *refs),
        out_shape=(
            pltpu.HBM((block, hidden), F32),
            jax.ShapeDtypeStruct((8, 128), F32),
        ),
        in_specs=[VMEM_SPEC] * (2 * n_dp),
        out_specs=(HBM_SPEC, VMEM_SPEC),
        scratch_shapes=[
            pltpu.VMEM((n_dp * group, block), BF),
            pltpu.VMEM((2, n_dp * group, hidden), BF),
            pltpu.VMEM((block, hidden), F32),
            pltpu.SemaphoreType.DMA((len(cuts),)),
        ],
        compiler_params=pltpu.CompilerParams(vmem_limit_bytes=32 << 20),
        cost_estimate=pl.CostEstimate(
            flops=2 * n_dp * group * block * hidden,
            bytes_accessed=4 * block * hidden,
            transcendentals=0,
        ),
        name="product",
    )(*columns, *packs)
    grad_normed = pl.pallas_call(
        lambda *refs: final_kernel(own, *refs),
        out_shape=jax.ShapeDtypeStruct((own, width), BF),
        in_specs=[VMEM_SPEC] * 4 + [ANY_SPEC],
        out_specs=VMEM_SPEC,
        compiler_params=pltpu.CompilerParams(vmem_limit_bytes=2 << 20),
        name="final_sum",
    )(chip, *pieces, token)
    return grad_normed, weight_grads


def solution(mesh):
    n_dp, n_node = mesh.shape["dp"], mesh.shape["node"]

    def shards(*arrays):
        normed, gate_weight = arrays[0], arrays[2]
        rows, width = normed.shape
        hidden = gate_weight.shape[1]
        fits = (
            n_dp == 4
            and n_node == 8
            and rows * n_node == 16
            and hidden % 256 == 0
            and hidden * width * 6 <= 46 << 20
            and width % (n_dp * 256) == 0
        )
        if fits:
            return shards_group((n_dp, n_node), *arrays)
        return shards_any(n_dp, *arrays)

    in_specs = (
        P(("dp", "node"), None),
        P(("dp", "node"), None),
        P(None, "node"),
        P(None, "node"),
        P("node", None),
    )
    out_specs = (P(("dp", "node"), None), P("dp", "node"))
    return jax.shard_map(shards, mesh=mesh, in_specs=in_specs, out_specs=out_specs, check_vma=False)
```
